32 devices in a mesh: energy: 4 (over y, x), block: 8 (over z, core).
Axes of the slice: x: 2, y: 2, z: 4, core: 2. Of those that a mesh axis runs over, the one named last changes fastest.
Arguments:
- g_less: bfloat16 [128, 8, 128, 128], P('energy', 'block'), may hold values from -6 to 6
- g_great: bfloat16 [128, 8, 128, 128], P('energy', 'block'), may hold values from -6 to 6
- coupling: bfloat16 [8, 3, 128, 128], P('block'), may hold values from -0.3125 to 0.3125
- coupling_mask: int32 [8, 2], P('block'), may hold values 0 or 1
Outputs:
- sigma_less: float32 [128, 8, 128, 128], P('energy', 'block')
The draws below stay inside these ranges and needn't reach their ends.
All inputs are finite; a program needn't handle non-finite values. No bound on the sum of `coupling_mask` on one device may be relied on, other than what follows from the above.
Results may differ from the reference program's by a relative error of at most 0.009.
Values may be sent and summed in bfloat16 or wider, within the bound.
No kernel may reach another device: no remote copies, remote signals or barrier semaphores. Data moves between devices by JAX's collectives and lax.ppermute only.
A program may use at most 64 MiB of HBM per device.

```python
import math
import jax
import jax.numpy as jnp
from jax import lax

ORB = 128
NE = 128
NB = 8


def plant(drawn, own_key, low, top_value):
    place = [jax.random.randint(jax.random.fold_in(own_key, axis), (), 0, length) for axis, length in enumerate(drawn.shape)]
    longest = drawn.shape.index(max(drawn.shape))
    beside = place[:longest] + [(place[longest] + 1) % drawn.shape[longest]] + place[longest + 1:]
    return drawn.at[tuple(place)].set(low).at[tuple(beside)].set(top_value)


def shard_levels(key, dims, split, low, largest):
    def one(dim, blocks):
        steps = jax.random.uniform(jax.random.fold_in(jax.random.fold_in(key, 6), dim), (blocks,), jnp.float32, low / len(split), largest / len(split))
        return jnp.repeat(jnp.exp(steps), dims[dim] // blocks).reshape((-1,) + (1,) * (len(dims) - dim - 1))

    gain = one(*split[0])
    for cut in split[1:]:
        gain = gain * one(*cut)
    return gain


def centred(own_key, shape, deviation, limit, shards=(), kind=jnp.bfloat16):
    drawn = jax.random.normal(own_key, shape, jnp.float32) * deviation
    if len(shards) > 0:
        drawn = shard_levels(own_key, shape, shards, -0.22, 0.18) * drawn
    return jnp.clip(drawn, min=-limit, max=limit).astype(kind)


def setup_inputs(seed: int = 0) -> dict:
    key_list = jax.random.split(jax.random.key(seed), 5)
    g_less = centred(key_list[0], (NE, NB, ORB, ORB), 1.0, 6.0, ((0, 4), (1, 8)))
    g_great = centred(key_list[1], (NE, NB, ORB, ORB), 1.0, 6.0, ((0, 4), (1, 8)))
    coupling = centred(key_list[2], (NB, 3, ORB, ORB), (3 * ORB) ** -0.5, 0.3125, ((0, 8),))
    coupling_mask = plant((jax.random.randint(key_list[3], (NB, 2), 0, 4) < 3).astype(jnp.int32), jax.random.fold_in(key_list[3], 1), 0, 1)
    return dict(g_less=g_less, g_great=g_great, coupling=coupling, coupling_mask=coupling_mask)


def lag_order(series):
    return jnp.concatenate([series[2 * NE - NE // 2:], series[:NE // 2]], axis=0)

def polarize(pair):
    lesser, greater = pair
    lesser = lesser.astype(jnp.float32).reshape(NE, ORB * ORB)
    greater = jnp.swapaxes(greater, 1, 2).astype(jnp.float32).reshape(NE, ORB * ORB)
    spectrum = jnp.fft.rfft(lesser, n=2 * NE, axis=0) * jnp.conj(jnp.fft.rfft(greater, n=2 * NE, axis=0))
    series = jnp.fft.irfft(spectrum, n=2 * NE, axis=0)
    return (lag_order(series) / math.sqrt(NE)).reshape(NE, ORB, ORB)

def reference(g_less, g_great, coupling, coupling_mask):
    less_blocks = jnp.moveaxis(g_less, 1, 0)
    great_blocks = jnp.moveaxis(g_great, 1, 0)
    pol = lax.map(polarize, (less_blocks, great_blocks))
    empty_rim = jnp.zeros((1, NE, ORB, ORB), pol.dtype)
    padded = jnp.concatenate([empty_rim, pol, empty_rim], axis=0)
    present = coupling_mask.astype(jnp.float32)
    highest = lax.Precision.HIGHEST

    def screen(index):
        couple = coupling[index].astype(jnp.float32)
        factors = jnp.stack([present[index, 0], jnp.ones((), present.dtype), present[index, 1]])
        accumulated = jnp.zeros((NE, ORB, ORB), jnp.float32)
        for offset in range(3):
            neighbour = lax.dynamic_index_in_dim(padded, index + offset, 0, keepdims=False)
            halfway = jnp.einsum('ij,ejk->eik', couple[offset], neighbour, precision=highest)
            accumulated = accumulated + factors[offset] * jnp.einsum('eik,lk->eil', halfway, couple[offset], precision=highest)
        return accumulated.astype(jnp.bfloat16)
    screened = lax.map(screen, jnp.arange(NB, dtype=jnp.int32))

    def selfenergy(pair):
        lesser, interaction = pair
        lesser = lesser.astype(jnp.float32).reshape(NE, ORB * ORB)
        interaction = interaction.astype(jnp.float32).reshape(NE, ORB * ORB)
        circular = jnp.concatenate([interaction[NE // 2:], jnp.zeros((NE, ORB * ORB), interaction.dtype), interaction[:NE // 2]], axis=0)
        spectrum = jnp.fft.rfft(lesser, n=2 * NE, axis=0) * jnp.fft.rfft(circular, n=2 * NE, axis=0)
        convolved = jnp.fft.irfft(spectrum, n=2 * NE, axis=0)[:NE]
        return (convolved / math.sqrt(NE)).reshape(NE, ORB, ORB)
    sigma = lax.map(selfenergy, (less_blocks, screened))
    return jnp.moveaxis(sigma, 0, 1).astype(jnp.float32)
```

```python
import functools
import math

import jax
import jax.numpy as jnp
import numpy as np
from jax import lax
from jax.experimental import pallas as pl
from jax.experimental.pallas import tpu as pltpu
from jax.sharding import PartitionSpec as P

BF16 = jnp.bfloat16
F32 = jnp.float32


def split(table):
    upper = table.astype(BF16)
    lower = (table - upper.astype(np.float32)).astype(BF16)
    return upper, lower


def tables(groups, e_dev):
    total = groups * e_dev
    length = 3 * total // 2
    omega = 2.0 * math.pi / length * (np.arange(length // 2) + 0.5)
    scale = 2.0 / (length * math.sqrt(total))
    energies = np.arange(total)
    lags = energies - total // 2

    def forward(points):
        angle = omega[:, None] * points[None, :]
        table = np.concatenate([np.cos(angle), np.sin(angle)], axis=0).astype(np.float32)
        return np.concatenate(split(table), axis=1)

    def backward(points):
        angle = points[:, None] * omega[None, :]
        table = np.concatenate([np.cos(angle), np.sin(angle)], axis=1) * scale
        return np.concatenate(split(table.astype(np.float32)), axis=0)

    def ordered(me):
        return np.concatenate([np.arange(e_dev) + (me ^ d) * e_dev for d in range(groups)])

    fwd_e = np.stack([forward(energies[ordered(me)]) for me in range(groups)])
    fwd_l = np.stack([forward(lags[ordered(me)]) for me in range(groups)])
    back_l = np.stack([backward(lags[ordered(me)]) for me in range(groups)])
    back_e = np.stack([backward(energies[ordered(me)]) for me in range(groups)])
    return fwd_e, fwd_l, back_l, back_e


def params():
    return pltpu.CompilerParams(vmem_limit_bytes=40 * 1024 * 1024)


def vmem():
    return pl.BlockSpec(memory_space=pltpu.VMEM)


def dot(a, b):
    return jnp.dot(a, b, preferred_element_type=F32)


def less_kernel(groups, me_ref, x_ref, *rest):
    outs, scratch = rest[:groups], rest[groups]
    e_dev, orbitals, _ = x_ref.shape
    rows = orbitals // groups
    me = me_ref[0]
    for d in range(groups):
        start = pl.multiple_of((me ^ d) * rows, rows)
        for e in range(e_dev):
            scratch[pl.ds(d * rows * e_dev + e, rows, stride=e_dev), :] = x_ref[
                e, pl.ds(start, rows), :
            ].astype(F32)
    for d in range(groups):
        outs[d][...] = (
            scratch[d * rows * e_dev : (d + 1) * rows * e_dev, :]
            .astype(BF16)
            .reshape(rows, e_dev, orbitals)
        )


def great_kernel(groups, me_ref, x_ref, *rest):
    outs, scratch = rest[:groups], rest[groups]
    e_dev, orbitals, _ = x_ref.shape
    rows = orbitals // groups
    me = me_ref[0]
    for e in range(e_dev):
        scratch[pl.ds(e, orbitals, stride=e_dev), :] = x_ref[e].astype(F32).T
    for d in range(groups):
        size = rows * e_dev
        start = pl.multiple_of((me ^ d) * size, size)
        outs[d][...] = (
            scratch[pl.ds(start, size), :].astype(BF16).reshape(rows, e_dev, orbitals)
        )


def prepare(kernel, me, x):
    e_dev, orbitals, _ = x.shape
    groups = lax.axis_size("energy")
    rows = orbitals // groups
    return pl.pallas_call(
        functools.partial(kernel, groups),
        out_shape=[jax.ShapeDtypeStruct((rows, e_dev, orbitals), BF16)] * groups,
        in_specs=[pl.BlockSpec(memory_space=pltpu.SMEM), vmem()],
        out_specs=[vmem()] * groups,
        scratch_shapes=[pltpu.VMEM((orbitals * e_dev, orbitals), F32)],
        compiler_params=params(),
    )(me, x)


def gathered(refs, i):
    pair = [
        jnp.concatenate([ref[i + h] for ref in refs], axis=0) for h in range(2)
    ]
    both = jnp.concatenate(pair, axis=1)
    return jnp.concatenate([both, both], axis=0)


def inverse(back, spectrum):
    both = dot(back, spectrum.astype(BF16))
    half = both.shape[0] // 2
    return both[:half] + both[half:]


def pol_kernel(groups, fwd_ref, back_ref, *refs):
    less, great = refs[:groups], refs[groups : 2 * groups]
    outs, scratch = refs[2 * groups : 3 * groups], refs[3 * groups]
    rows, e_dev, orbitals = less[0].shape
    freq = fwd_ref.shape[0] // 2
    fwd, back = fwd_ref[...], back_ref[...]
    total = groups * e_dev
    for i in range(0, rows, 2):
        a = dot(fwd, gathered(less, i))
        b = dot(fwd, gathered(great, i))
        real = a[:freq] * b[:freq] + a[freq:] * b[freq:]
        imag = a[freq:] * b[:freq] - a[:freq] * b[freq:]
        pol = inverse(back, jnp.concatenate([real, imag], axis=0))
        for h in range(2):
            scratch[pl.ds(i + h, total, stride=rows), :] = pol[
                :, h * orbitals : (h + 1) * orbitals
            ]
    for d in range(groups):
        size = e_dev * rows
        outs[d][...] = (
            scratch[d * size : (d + 1) * size, :].astype(BF16).reshape(e_dev, rows, orbitals)
        )


def sigma_kernel(groups, fwd_e_ref, fwd_l_ref, back_ref, *refs):
    less, inter = refs[:groups], refs[groups : 2 * groups]
    outs = refs[2 * groups :]
    rows, e_dev, orbitals = less[0].shape
    freq = fwd_e_ref.shape[0] // 2
    fwd_e, fwd_l, back = fwd_e_ref[...], fwd_l_ref[...], back_ref[...]
    for i in range(0, rows, 2):
        a = dot(fwd_e, gathered(less, i))
        b = dot(fwd_l, gathered(inter, i))
        real = a[:freq] * b[:freq] - a[freq:] * b[freq:]
        imag = a[freq:] * b[:freq] + a[:freq] * b[freq:]
        sigma = inverse(back, jnp.concatenate([real, imag], axis=0)).astype(BF16)
        for h in range(2):
            for d in range(groups):
                outs[d][i + h] = sigma[
                    d * e_dev : (d + 1) * e_dev, h * orbitals : (h + 1) * orbitals
                ]


def assemble_kernel(groups, me_ref, *refs):
    ins, out = refs[:groups], refs[groups]
    rows = ins[0].shape[1]
    me = me_ref[0]
    for d in range(groups):
        start = pl.multiple_of((me ^ d) * rows, rows)
        out[:, pl.ds(start, rows), :] = ins[d][...]


def screen_kernel(groups, me_ref, mask_ref, v_ref, vt_ref, before, own, after, *refs):
    outs, scratch = refs[:groups], refs[groups]
    lags, orbitals, _ = own.shape
    rows = orbitals // groups
    me = me_ref[0]
    left = [v_ref[t] for t in range(3)]
    right = jnp.concatenate(
        [
            vt_ref[0] * mask_ref[0].astype(F32).astype(BF16),
            vt_ref[1],
            vt_ref[2] * mask_ref[1].astype(F32).astype(BF16),
        ],
        axis=0,
    )
    for k in range(0, lags, 2):
        half = [
            dot(left[t], jnp.concatenate([ref[k], ref[k + 1]], axis=1)).astype(BF16)
            for t, ref in enumerate((before, own, after))
        ]
        for h in range(2):
            cols = slice(h * orbitals, (h + 1) * orbitals)
            term = dot(jnp.concatenate([x[:, cols] for x in half], axis=1), right)
            scratch[pl.ds(k + h, orbitals, stride=lags), :] = term
    for d in range(groups):
        size = rows * lags
        start = pl.multiple_of((me ^ d) * size, size)
        outs[d][...] = (
            scratch[pl.ds(start, size), :].astype(BF16).reshape(rows, lags, orbitals)
        )


def final_kernel(groups, me_ref, *refs):
    ins, out = refs[:groups], refs[groups]
    rows, e_dev, orbitals = ins[0].shape
    me = me_ref[0]
    for d in range(groups):
        for i in range(rows):
            out[pl.ds((me ^ d) * rows + i, e_dev, stride=orbitals), :] = ins[d][i].astype(F32)


def exchange(parts):
    groups = lax.axis_size("energy")
    moved = [parts[0]]
    for d in range(1, groups):
        moved.append(lax.ppermute(parts[d], "energy", [(i, i ^ d) for i in range(groups)]))
    return moved


def shards(g_less, g_great, coupling, coupling_mask):
    e_dev, _, orbitals, _ = g_less.shape
    groups = lax.axis_size("energy")
    peers = lax.axis_size("block")
    rows = orbitals // groups
    total = e_dev * groups
    index = lax.axis_index("energy")
    me = index.astype(jnp.int32)[None]
    fwd_e, fwd_l, back_l, back_e = [
        lax.dynamic_index_in_dim(jnp.asarray(t), index, 0, keepdims=False)
        for t in tables(groups, e_dev)
    ]
    smem = pl.BlockSpec(memory_space=pltpu.SMEM)
    less = exchange(prepare(less_kernel, me, g_less.reshape(e_dev, orbitals, orbitals)))
    great = exchange(prepare(great_kernel, me, g_great.reshape(e_dev, orbitals, orbitals)))
    pol = pl.pallas_call(
        functools.partial(pol_kernel, groups),
        out_shape=[jax.ShapeDtypeStruct((e_dev, rows, orbitals), BF16)] * groups,
        in_specs=[vmem()] * (2 + 2 * groups),
        out_specs=[vmem()] * groups,
        scratch_shapes=[pltpu.VMEM((total * rows, orbitals), F32)],
        compiler_params=params(),
    )(fwd_e, back_l, *less, *great)
    pol = exchange(pol)
    own = pl.pallas_call(
        functools.partial(assemble_kernel, groups),
        out_shape=jax.ShapeDtypeStruct((e_dev, orbitals, orbitals), BF16),
        in_specs=[smem] + [vmem()] * groups,
        out_specs=vmem(),
        compiler_params=params(),
    )(me, *pol)
    before = lax.ppermute(own, "block", [(i, i + 1) for i in range(peers - 1)])
    after = lax.ppermute(own, "block", [(i + 1, i) for i in range(peers - 1)])
    v = coupling[0]
    vt = jnp.swapaxes(v, 1, 2)
    inter = pl.pallas_call(
        functools.partial(screen_kernel, groups),
        out_shape=[jax.ShapeDtypeStruct((rows, e_dev, orbitals), BF16)] * groups,
        in_specs=[smem, smem] + [vmem()] * 5,
        out_specs=[vmem()] * groups,
        scratch_shapes=[pltpu.VMEM((orbitals * e_dev, orbitals), F32)],
        compiler_params=params(),
    )(me, coupling_mask[0], v, vt, before, own, after)
    inter = exchange(inter)
    sigma = pl.pallas_call(
        functools.partial(sigma_kernel, groups),
        out_shape=[jax.ShapeDtypeStruct((rows, e_dev, orbitals), BF16)] * groups,
        in_specs=[vmem()] * (3 + 2 * groups),
        out_specs=[vmem()] * groups,
        compiler_params=params(),
    )(fwd_e, fwd_l, back_e, *less, *inter)
    sigma = exchange(sigma)
    out = pl.pallas_call(
        functools.partial(final_kernel, groups),
        out_shape=jax.ShapeDtypeStruct((e_dev * orbitals, orbitals), F32),
        in_specs=[smem] + [vmem()] * groups,
        out_specs=vmem(),
        compiler_params=params(),
    )(me, *sigma)
    return out.reshape(e_dev, 1, orbitals, orbitals)


def solution(mesh):
    return jax.shard_map(
        shards,
        mesh=mesh,
        in_specs=(
            P("energy", "block", None, None),
            P("energy", "block", None, None),
            P("block", None, None, None),
            P("block", None),
        ),
        out_specs=P("energy", "block", None, None),
        check_vma=False,
    )
```

```python
import functools
import math

import jax
import jax.numpy as jnp
import numpy as np
from jax import lax
from jax.experimental import pallas as pl
from jax.experimental.pallas import tpu as pltpu
from jax.sharding import PartitionSpec as P

BF16 = jnp.bfloat16
F32 = jnp.float32
WIDE = 8


def split(table):
    upper = table.astype(BF16)
    lower = (table - upper.astype(np.float32)).astype(BF16)
    return upper, lower


def tables(groups, e_dev):
    total = groups * e_dev
    length = 3 * total // 2
    omega = 2.0 * math.pi / length * (np.arange(length // 2) + 0.5)
    scale = 2.0 / (length * math.sqrt(total))
    energies = np.arange(total)
    lags = energies - total // 2

    def forward(points):
        angle = omega[:, None] * points[None, :]
        table = np.concatenate([np.cos(angle), np.sin(angle)], axis=0).astype(np.float32)
        return np.concatenate(split(table), axis=1)

    def backward(points):
        angle = points[:, None] * omega[None, :]
        table = np.concatenate([np.cos(angle), np.sin(angle)], axis=1) * scale
        return np.concatenate(split(table.astype(np.float32)), axis=0)

    def ordered(me):
        return np.concatenate([np.arange(e_dev) + (me ^ d) * e_dev for d in range(groups)])

    fwd_e = np.stack([forward(energies[ordered(me)]) for me in range(groups)])
    fwd_l = np.stack([forward(lags[ordered(me)]) for me in range(groups)])
    back_l = np.stack([backward(lags[ordered(me)]) for me in range(groups)])
    back_e = np.stack([backward(energies[ordered(me)]) for me in range(groups)])
    return fwd_e, fwd_l, back_l, back_e


def params():
    return pltpu.CompilerParams(vmem_limit_bytes=12 * 1024 * 1024)


def vmem():
    return pl.BlockSpec(memory_space=pltpu.VMEM)


def dot(a, b):
    return jnp.dot(a, b, preferred_element_type=F32)


def prepare_kernel(groups, transposed, me_ref, hbm, *rest):
    outs = rest[:groups]
    x_ref, scratch, sems = rest[groups:]
    e_dev, orbitals, _ = x_ref.shape
    rows = orbitals // groups
    me = me_ref[0]
    span = e_dev // sems.shape[0]
    copies = []
    for p in range(sems.shape[0]):
        part = pl.ds(p * span, span)
        copies.append(pltpu.make_async_copy(hbm.at[part], x_ref.at[part], sems.at[p]))
        copies[p].start()
    for p, copy in enumerate(copies):
        copy.wait()
        for e in range(p * span, (p + 1) * span):
            x = x_ref[e].astype(F32)
            scratch[pl.ds(e, orbitals, stride=e_dev), :] = x.T if transposed else x
    size = rows * e_dev
    for d in range(groups):
        part = scratch[pl.ds(pl.multiple_of((me ^ d) * size, size), size), :]
        outs[d][...] = part.astype(BF16).reshape(rows, e_dev, orbitals)


def gathered(refs, i):
    both = jnp.concatenate(
        [jnp.concatenate([ref[i + h] for ref in refs], axis=0) for h in range(WIDE)], axis=1
    )
    return jnp.concatenate([both, both], axis=0)


def inverse(back, spectrum):
    both = dot(back, spectrum.astype(BF16))
    half = both.shape[0] // 2
    return both[:half] + both[half:]


def spectrum_kernel(fwd_ref, *refs):
    less, out = refs[:-1], refs[-1]
    fwd = fwd_ref[...]
    for n in range(out.shape[0]):
        out[n] = dot(fwd, gathered(less, n * WIDE))


def pol_kernel(groups, halves, fwd_ref, back_ref, less_ref, *refs):
    great, outs, scratch = refs[:groups], refs[groups:-1], refs[-1]
    rows, e_dev, orbitals = great[0].shape
    freq = fwd_ref.shape[0] // 2
    fwd, back = fwd_ref[...], back_ref[...]
    total = groups * e_dev
    for n in range(less_ref.shape[0]):
        a = less_ref[n]
        b = dot(fwd, gathered(great, n * WIDE))
        real = a[:freq] * b[:freq] + a[freq:] * b[freq:]
        imag = a[freq:] * b[:freq] - a[:freq] * b[freq:]
        pol = inverse(back, jnp.concatenate([real, imag], axis=0))
        for h in range(WIDE):
            scratch[pl.ds(n * WIDE + h, total, stride=rows), :] = pol[
                :, h * orbitals : (h + 1) * orbitals
            ]
    lags = e_dev // halves
    size = lags * rows
    for h in range(halves):
        for d in range(groups):
            start = (d * halves + h) * size
            outs[h * groups + d][...] = (
                scratch[start : start + size, :].astype(BF16).reshape(lags, rows, orbitals)
            )


def sigma_kernel(groups, halves, fwd_l_ref, back_ref, less_ref, *refs):
    inter, outs = refs[: groups * halves], refs[groups * halves :]
    count, e_dev, orbitals = outs[0].shape
    inter = [inter[h * groups + d] for d in range(groups) for h in range(halves)]
    freq = fwd_l_ref.shape[0] // 2
    fwd_l, back = fwd_l_ref[...], back_ref[...]
    for n in range(less_ref.shape[0]):
        a = less_ref[n]
        b = dot(fwd_l, gathered(inter, n * WIDE))
        real = a[:freq] * b[:freq] - a[freq:] * b[freq:]
        imag = a[freq:] * b[:freq] + a[:freq] * b[freq:]
        sigma = inverse(back, jnp.concatenate([real, imag], axis=0)).astype(BF16)
        for h in range(WIDE):
            c, i = divmod(n * WIDE + h, count)
            for d in range(groups):
                outs[c * groups + d][i] = sigma[
                    d * e_dev : (d + 1) * e_dev, h * orbitals : (h + 1) * orbitals
                ]


def assemble_kernel(groups, me_ref, *refs):
    ins, out = refs[:groups], refs[groups]
    rows = ins[0].shape[1]
    me = me_ref[0]
    for d in range(groups):
        start = pl.multiple_of((me ^ d) * rows, rows)
        out[:, pl.ds(start, rows), :] = ins[d][...]


def diagonal(a, b):
    zero = jnp.zeros_like(a)
    return jnp.concatenate(
        [jnp.concatenate([a, zero], axis=1), jnp.concatenate([zero, b], axis=1)], axis=0
    )


def setup_kernel(count, me_ref, odd_ref, mask_ref, v_ref, *refs):
    sources, outs = refs[:count], refs[count : 2 * count]
    near_left, near_right, far_left, far_right = refs[2 * count : -1]
    sems = refs[-1]
    copies = [
        pltpu.make_async_copy(src.at[me_ref[0]], dst, sems.at[n])
        for n, (src, dst) in enumerate(zip(sources, outs))
    ]
    for copy in copies:
        copy.start()
    odd = odd_ref[0]
    own, near, far = v_ref[1], v_ref[2 - 2 * odd], v_ref[2 * odd]

    def masked(v, t):
        return (v.astype(F32).T * mask_ref[t].astype(F32)).astype(BF16)

    near_left[...] = jnp.concatenate([own, near], axis=1)
    near_right[...] = diagonal(own.astype(F32).T.astype(BF16), masked(near, 1 - odd))
    far_left[...] = far
    far_right[...] = masked(far, odd)
    for copy in copies:
        copy.wait()


def near_kernel(left, right, own, near, out):
    lags, n, _ = own.shape
    both = jnp.concatenate([own[...].reshape(lags * n, n), near[...].reshape(lags * n, n)], axis=1)
    half = dot(both, right[...]).astype(BF16)
    half = jnp.concatenate(
        [
            jnp.concatenate([half[k * n : k * n + n, :n], half[k * n : k * n + n, n:]], axis=0)
            for k in range(lags)
        ],
        axis=1,
    )
    terms = dot(left[...], half)
    for k in range(lags):
        out[k] = terms[:, k * n : k * n + n]


def far_kernel(groups, me_ref, left, right, partial, far, *refs):
    outs, scratch = refs[:groups], refs[groups]
    lags, n, _ = far.shape
    rows = n // groups
    me = me_ref[0]
    half = dot(far[...].reshape(lags * n, n), right[...]).astype(BF16)
    half = jnp.concatenate([half[k * n : k * n + n] for k in range(lags)], axis=1)
    terms = dot(left[...], half)
    for k in range(lags):
        scratch[pl.ds(k, n, stride=lags), :] = partial[k] + terms[:, k * n : k * n + n]
    size = rows * lags
    for d in range(groups):
        place = pl.ds(pl.multiple_of((me ^ d) * size, size), size)
        outs[d][...] = scratch[place, :].astype(BF16).reshape(rows, lags, n)


def final_kernel(groups, first, me_ref, *refs):
    ins, out, scratch, sems = refs[:groups], refs[-3], refs[-2], refs[-1]
    count, e_dev, orbitals = ins[0].shape
    rows = orbitals // groups
    me = me_ref[0]
    copies = []
    for d in range(groups):
        for i in range(count):
            scratch[d, pl.ds(i, e_dev, stride=count), :] = ins[d][i].astype(F32)
        start = pl.multiple_of((me ^ d) * rows + first, 8)
        copies.append(
            pltpu.make_async_copy(
                scratch.at[d].reshape(e_dev, count, orbitals),
                out.at[:, pl.ds(start, count), :],
                sems.at[d],
            )
        )
        copies[-1].start()
    for copy in copies:
        copy.wait()


def exchange(parts):
    groups = lax.axis_size("energy")
    moved = [parts[0]]
    for d in range(1, groups):
        moved.append(lax.ppermute(parts[d], "energy", [(i, i ^ d) for i in range(groups)]))
    return moved


def call(kernel, out_shape, specs, *args, scratch=(), **kwargs):
    return pl.pallas_call(
        kernel,
        out_shape=out_shape,
        in_specs=specs,
        scratch_shapes=list(scratch),
        compiler_params=params(),
        **kwargs,
    )(*args)


def shards(g_less, g_great, coupling, coupling_mask):
    e_dev, _, orbitals, _ = g_less.shape
    groups = lax.axis_size("energy")
    peers = lax.axis_size("block")
    rows = orbitals // groups
    total = e_dev * groups
    halves = 2 if e_dev % 32 == 0 else 1
    lags = e_dev // halves
    index = lax.axis_index("energy")
    me = index.astype(jnp.int32)[None]
    odd = (lax.axis_index("block") % 2).astype(jnp.int32)[None]
    smem = pl.BlockSpec(memory_space=pltpu.SMEM)
    hbm = pl.BlockSpec(memory_space=pltpu.HBM)

    def shape(*dims, dtype=BF16):
        return jax.ShapeDtypeStruct(dims, dtype)

    less = g_less.reshape(e_dev, orbitals, orbitals)
    great = g_great.reshape(e_dev, orbitals, orbitals)
    less, great = [pltpu.with_memory_space_constraint(x, pltpu.HBM) for x in (less, great)]

    def prepared(x, transposed):
        parts = call(
            functools.partial(prepare_kernel, groups, transposed),
            [shape(rows, e_dev, orbitals)] * groups,
            [smem, hbm],
            me,
            x,
            out_specs=[vmem()] * groups,
            scratch=[
                pltpu.VMEM((e_dev, orbitals, orbitals), BF16),
                pltpu.VMEM((orbitals * e_dev, orbitals), F32),
                pltpu.SemaphoreType.DMA((4,)),
            ],
        )
        return exchange(parts)

    less = prepared(less, False)
    great = prepared(great, True)
    stacks = [pltpu.with_memory_space_constraint(jnp.asarray(t), pltpu.HBM) for t in tables(groups, e_dev)]
    square = (orbitals, orbitals)
    fwd_e, fwd_l, back_l, back_e, near_left, near_right, far_left, far_right = call(
        functools.partial(setup_kernel, len(stacks)),
        [shape(*t.shape[1:]) for t in stacks]
        + [shape(orbitals, 2 * orbitals), shape(2 * orbitals, 2 * orbitals)]
        + [shape(*square), shape(*square)],
        [smem, smem, smem, vmem()] + [hbm] * len(stacks),
        me,
        odd,
        coupling_mask[0],
        coupling[0],
        *stacks,
        out_specs=[vmem()] * (len(stacks) + 4),
        scratch=[pltpu.SemaphoreType.DMA((len(stacks),))],
    )
    less = call(
        spectrum_kernel,
        shape(rows // WIDE, fwd_e.shape[0], WIDE * orbitals, dtype=F32),
        [vmem()] * (1 + groups),
        fwd_e,
        *less,
        out_specs=vmem(),
    )
    pol = call(
        functools.partial(pol_kernel, groups, halves),
        [shape(lags, rows, orbitals)] * (halves * groups),
        [vmem()] * (3 + groups),
        fwd_e,
        back_l,
        less,
        *great,
        out_specs=[vmem()] * (halves * groups),
        scratch=[pltpu.VMEM((total * rows, orbitals), F32)],
    )
    pol = [exchange(pol[h * groups : (h + 1) * groups]) for h in range(halves)]

    near_pairs = [(b, b ^ 1) for b in range(peers) if b ^ 1 < peers]
    far_pairs = [(b, ((b + 1) ^ 1) - 1) for b in range(1, peers) if ((b + 1) ^ 1) - 1 < peers]
    inter = []
    for h in range(halves):
        own = call(
            functools.partial(assemble_kernel, groups),
            shape(lags, orbitals, orbitals),
            [smem] + [vmem()] * groups,
            me,
            *pol[h],
            out_specs=vmem(),
        )
        far = lax.ppermute(own, "block", far_pairs)
        near = lax.ppermute(own, "block", near_pairs)
        partial = call(
            near_kernel,
            shape(lags, orbitals, orbitals, dtype=F32),
            [vmem()] * 4,
            near_left,
            near_right,
            own,
            near,
            out_specs=vmem(),
        )
        parts = call(
            functools.partial(far_kernel, groups),
            [shape(rows, lags, orbitals)] * groups,
            [smem] + [vmem()] * 4,
            me,
            far_left,
            far_right,
            partial,
            far,
            out_specs=[vmem()] * groups,
            scratch=[pltpu.VMEM((orbitals * lags, orbitals), F32)],
        )
        inter += exchange(parts)

    steps = 2 if rows % 32 == 0 else 1
    count = rows // steps
    sigma = call(
        functools.partial(sigma_kernel, groups, halves),
        [shape(count, e_dev, orbitals)] * (groups * steps),
        [vmem()] * (3 + groups * halves),
        fwd_l,
        back_e,
        less,
        *inter,
        out_specs=[vmem()] * (groups * steps),
    )
    sigma = [
        (c * count, count, exchange(sigma[c * groups : (c + 1) * groups])) for c in range(steps)
    ]
    out = []
    for first, count, parts in sigma:
        out = [
            call(
                functools.partial(final_kernel, groups, first),
                shape(e_dev, orbitals, orbitals, dtype=F32),
                [smem] + [vmem()] * groups + [hbm] * len(out),
                me,
                *parts,
                *out,
                out_specs=hbm,
                scratch=[
                    pltpu.VMEM((groups, e_dev * count, orbitals), F32),
                    pltpu.SemaphoreType.DMA((groups,)),
                ],
                input_output_aliases={1 + groups: 0} if out else {},
            )
        ]
    return out[0].reshape(e_dev, 1, orbitals, orbitals)


def solution(mesh):
    return jax.shard_map(
        shards,
        mesh=mesh,
        in_specs=(
            P("energy", "block", None, None),
            P("energy", "block", None, None),
            P("block", None, None, None),
            P("block", None),
        ),
        out_specs=P("energy", "block", None, None),
        check_vma=False,
    )
```

```python
import functools
import math

import jax
import jax.numpy as jnp
import numpy as np
from jax import lax
from jax.experimental import pallas as pl
from jax.experimental.pallas import tpu as pltpu
from jax.sharding import PartitionSpec as P

BF16 = jnp.bfloat16
F32 = jnp.float32
WIDE = 8


def split(table):
    upper = table.astype(BF16)
    lower = (table - upper.astype(np.float32)).astype(BF16)
    return upper, lower


def tables(groups, e_dev):
    total = groups * e_dev
    length = 3 * total // 2
    omega = 2.0 * math.pi / length * (np.arange(length // 2) + 0.5)
    scale = 2.0 / (length * math.sqrt(total))
    energies = np.arange(total)
    lags = energies - total // 2

    def forward(points):
        angle = omega[:, None] * points[None, :]
        table = np.concatenate([np.cos(angle), np.sin(angle)], axis=0).astype(np.float32)
        return np.concatenate(split(table), axis=1)

    def backward(points):
        angle = points[:, None] * omega[None, :]
        table = np.concatenate([np.cos(angle), np.sin(angle)], axis=1) * scale
        return np.concatenate(split(table.astype(np.float32)), axis=0)

    def ordered(me):
        return np.concatenate([np.arange(e_dev) + (me ^ d) * e_dev for d in range(groups)])

    fwd_e = np.stack([forward(energies[ordered(me)]) for me in range(groups)])
    fwd_l = np.stack([forward(lags[ordered(me)]) for me in range(groups)])
    back_l = np.stack([backward(lags[ordered(me)]) for me in range(groups)])
    back_e = np.stack([backward(energies[ordered(me)]) for me in range(groups)])
    return fwd_e, fwd_l, back_l, back_e


def params():
    return pltpu.CompilerParams(vmem_limit_bytes=12 * 1024 * 1024)


def vmem():
    return pl.BlockSpec(memory_space=pltpu.VMEM)


def dot(a, b):
    return jnp.dot(a, b, preferred_element_type=F32)


def slice_kernel(groups, me_ref, hbm, *rest):
    outs, sems = rest[:groups], rest[groups]
    rows = outs[0].shape[1]
    copies = []
    for d in range(groups):
        place = pl.ds(pl.multiple_of((me_ref[0] ^ d) * rows, rows), rows)
        copies.append(pltpu.make_async_copy(hbm.at[:, place], outs[d], sems.at[d]))
        copies[d].start()
    for copy in copies:
        copy.wait()


def turn_kernel(groups, counts, me_ref, hbm, *rest):
    outs = rest[: groups * len(counts)]
    x_ref, scratch, sems = rest[groups * len(counts) :]
    e_dev, orbitals, _ = x_ref.shape
    rows = orbitals // groups
    me = me_ref[0]
    span = e_dev // sems.shape[0]
    copies = []
    for p in range(sems.shape[0]):
        part = pl.ds(p * span, span)
        copies.append(pltpu.make_async_copy(hbm.at[part], x_ref.at[part], sems.at[p]))
        copies[p].start()
    for p, copy in enumerate(copies):
        copy.wait()
        for e in range(p * span, (p + 1) * span):
            scratch[pl.ds(e, orbitals, stride=e_dev), :] = x_ref[e].astype(F32).T
    first = 0
    for c, count in enumerate(counts):
        for d in range(groups):
            start = pl.multiple_of(((me ^ d) * rows + first) * e_dev, 8)
            part = scratch[pl.ds(start, count * e_dev), :]
            outs[c * groups + d][...] = part.astype(BF16).reshape(count, e_dev, orbitals)
        first += count


def gathered(refs, i):
    both = jnp.concatenate(
        [jnp.concatenate([ref[i + h] for ref in refs], axis=0) for h in range(WIDE)], axis=1
    )
    return jnp.concatenate([both, both], axis=0)


def inverse(back, spectrum):
    both = dot(back, spectrum.astype(BF16))
    half = both.shape[0] // 2
    return both[:half] + both[half:]


def spectrum_kernel(fwd_ref, *refs):
    less, out, scratch = refs[:-2], refs[-2], refs[-1]
    e_dev, rows, orbitals = less[0].shape
    size = e_dev * rows
    for d, part in enumerate(less):
        scratch[d * size : (d + 1) * size, :] = part[...].astype(F32).reshape(size, orbitals)
    fwd = fwd_ref[...]
    total = e_dev * len(less)
    for n in range(out.shape[0]):
        both = jnp.concatenate(
            [scratch[pl.ds(n * WIDE + h, total, stride=rows), :] for h in range(WIDE)], axis=1
        ).astype(BF16)
        out[n] = dot(fwd, jnp.concatenate([both, both], axis=0))


def pol_kernel(groups, halves, first, earlier, fwd_ref, back_ref, less_ref, *refs):
    great, before = refs[:groups], refs[groups : groups + earlier]
    outs, scratch = refs[groups + earlier : -1], refs[-1]
    count, e_dev, orbitals = great[0].shape
    freq = fwd_ref.shape[0] // 2
    fwd, back = fwd_ref[...], back_ref[...]
    total = groups * e_dev
    for i in range(0, count, WIDE):
        a = less_ref[(first + i) // WIDE]
        b = dot(fwd, gathered(great, i))
        real = a[:freq] * b[:freq] + a[freq:] * b[freq:]
        imag = a[freq:] * b[:freq] - a[:freq] * b[freq:]
        pol = inverse(back, jnp.concatenate([real, imag], axis=0))
        for h in range(WIDE):
            scratch[pl.ds(i + h, total, stride=count), :] = pol[
                :, h * orbitals : (h + 1) * orbitals
            ]
    if len(outs) == 1:
        outs[0][...] = scratch[...].astype(BF16).reshape(total, count, orbitals)
        return
    lags = e_dev // halves
    for h in range(halves):
        for d in range(groups):
            out = outs[h * groups + d]
            start = d * e_dev + h * lags
            at = 0
            for ref in before:
                out[:, at : at + ref.shape[1], :] = ref[start : start + lags]
                at += ref.shape[1]
            out[:, first:, :] = (
                scratch[start * count : (start + lags) * count, :]
                .astype(BF16)
                .reshape(lags, count, orbitals)
            )


def sigma_kernel(groups, halves, fwd_l_ref, back_ref, less_ref, *refs):
    inter, outs = refs[: groups * halves], refs[groups * halves :]
    e_dev, orbitals = outs[0].shape[1:]
    inter = [inter[h * groups + d] for d in range(groups) for h in range(halves)]
    freq = fwd_l_ref.shape[0] // 2
    fwd_l, back = fwd_l_ref[...], back_ref[...]
    for n in range(less_ref.shape[0]):
        a = less_ref[n]
        b = dot(fwd_l, gathered(inter, n * WIDE))
        real = a[:freq] * b[:freq] - a[freq:] * b[freq:]
        imag = a[freq:] * b[:freq] + a[:freq] * b[freq:]
        sigma = inverse(back, jnp.concatenate([real, imag], axis=0)).astype(BF16)
        for h in range(WIDE):
            for d in range(groups):
                outs[d][n * WIDE + h] = sigma[
                    d * e_dev : (d + 1) * e_dev, h * orbitals : (h + 1) * orbitals
                ]


def assemble_kernel(*refs):
    ins, out = refs[:-1], refs[-1]
    rows = ins[0].shape[1]
    for d, part in enumerate(ins):
        out[:, d * rows : (d + 1) * rows, :] = part[...]


def diagonal(a, b):
    zero = jnp.zeros_like(a)
    return jnp.concatenate(
        [jnp.concatenate([a, zero], axis=1), jnp.concatenate([zero, b], axis=1)], axis=0
    )


def setup_kernel(groups, count, me_ref, odd_ref, mask_ref, v_ref, *refs):
    sources, outs = refs[:count], refs[count : 2 * count]
    near_left, near_right, far_left, far_right, scratch, sems = refs[2 * count :]
    me = me_ref[0]
    copies = [
        pltpu.make_async_copy(src.at[me], dst, sems.at[n])
        for n, (src, dst) in enumerate(zip(sources, outs))
    ]
    for copy in copies:
        copy.start()
    odd = odd_ref[0]
    scratch[0] = v_ref[1].astype(F32).T
    scratch[1] = v_ref[2 - 2 * odd].astype(F32).T
    scratch[2] = v_ref[2 * odd].astype(F32).T
    rows = scratch.shape[1] // groups

    def ordered(n):
        parts = [
            scratch[n, pl.ds(pl.multiple_of((me ^ d) * rows, rows), rows), :] for d in range(groups)
        ]
        return jnp.concatenate(parts, axis=0).T.astype(BF16)

    def masked(n, t):
        return (scratch[n] * mask_ref[t].astype(F32)).astype(BF16)

    near_left[...] = jnp.concatenate([ordered(0), ordered(1)], axis=1)
    near_right[...] = diagonal(scratch[0].astype(BF16), masked(1, 1 - odd))
    far_left[...] = ordered(2)
    far_right[...] = masked(2, odd)
    for copy in copies:
        copy.wait()


def near_kernel(left, right, own, near, out):
    lags, n, _ = own.shape
    both = jnp.concatenate([own[...].reshape(lags * n, n), near[...].reshape(lags * n, n)], axis=1)
    half = dot(both, right[...]).astype(BF16)
    half = jnp.concatenate(
        [
            jnp.concatenate([half[k * n : k * n + n, :n], half[k * n : k * n + n, n:]], axis=0)
            for k in range(lags)
        ],
        axis=1,
    )
    terms = dot(left[...], half)
    for k in range(lags):
        out[k] = terms[:, k * n : k * n + n]


def far_kernel(groups, me_ref, left, right, partial, far, *refs):
    outs, scratch = refs[:groups], refs[groups]
    lags, n, _ = partial.shape
    rows = n // groups
    me = me_ref[0]
    half = dot(far[...].reshape(lags * n, n), right[...]).astype(BF16)
    half = jnp.concatenate([half[k * n : k * n + n] for k in range(lags)], axis=1)
    terms = dot(left[...], half)
    for k in range(lags):
        scratch[pl.ds(k, n, stride=lags), :] = partial[k] + terms[:, k * n : k * n + n]
    size = rows * lags
    for d in range(groups):
        place = pl.ds(pl.multiple_of((me ^ d) * size, size), size)
        outs[d][...] = scratch[place, :].astype(BF16).reshape(rows, lags, n)


def final_kernel(groups, which, me_ref, *refs):
    ins, out, scratch, sems = refs[: len(which)], refs[-3], refs[-2], refs[-1]
    rows, e_dev, orbitals = ins[0].shape
    me = me_ref[0]
    copies = []
    for n, d in enumerate(which):
        for i in range(rows):
            scratch[n, pl.ds(i, e_dev, stride=rows), :] = ins[n][i].astype(F32)
        start = pl.multiple_of((me ^ d) * rows, rows)
        copies.append(
            pltpu.make_async_copy(
                scratch.at[n].reshape(e_dev, rows, orbitals),
                out.at[:, pl.ds(start, rows), :],
                sems.at[n],
            )
        )
        copies[-1].start()
    for copy in copies:
        copy.wait()


def exchange(parts):
    groups = lax.axis_size("energy")
    moved = [parts[0]]
    for d in range(1, groups):
        moved.append(lax.ppermute(parts[d], "energy", [(i, i ^ d) for i in range(groups)]))
    return moved


def call(kernel, out_shape, specs, *args, scratch=(), **kwargs):
    return pl.pallas_call(
        kernel,
        out_shape=out_shape,
        in_specs=specs,
        scratch_shapes=list(scratch),
        compiler_params=params(),
        **kwargs,
    )(*args)


def shards(g_less, g_great, coupling, coupling_mask):
    e_dev, _, orbitals, _ = g_less.shape
    groups = lax.axis_size("energy")
    peers = lax.axis_size("block")
    rows = orbitals // groups
    total = e_dev * groups
    halves = 2 if e_dev % 32 == 0 else 1
    lags = e_dev // halves
    index = lax.axis_index("energy")
    me = index.astype(jnp.int32)[None]
    odd = (lax.axis_index("block") % 2).astype(jnp.int32)[None]
    smem = pl.BlockSpec(memory_space=pltpu.SMEM)
    hbm = pl.BlockSpec(memory_space=pltpu.HBM)

    def shape(*dims, dtype=BF16):
        return jax.ShapeDtypeStruct(dims, dtype)

    less = g_less.reshape(e_dev, orbitals, orbitals)
    great = g_great.reshape(e_dev, orbitals, orbitals)
    less, great = [pltpu.with_memory_space_constraint(x, pltpu.HBM) for x in (less, great)]

    parts = [shape(e_dev, rows, orbitals)] * groups
    less = call(
        functools.partial(slice_kernel, groups),
        parts,
        [smem, hbm],
        me,
        less,
        out_specs=[vmem()] * groups,
        scratch=[pltpu.SemaphoreType.DMA((groups,))],
    )
    less = exchange(less)
    stacks = [pltpu.with_memory_space_constraint(jnp.asarray(t), pltpu.HBM) for t in tables(groups, e_dev)]
    square = (orbitals, orbitals)
    fwd_e, fwd_l, back_l, back_e, near_left, near_right, far_left, far_right = call(
        functools.partial(setup_kernel, groups, len(stacks)),
        [shape(*t.shape[1:]) for t in stacks]
        + [shape(orbitals, 2 * orbitals), shape(2 * orbitals, 2 * orbitals)]
        + [shape(*square), shape(*square)],
        [smem, smem, smem, vmem()] + [hbm] * len(stacks),
        me,
        odd,
        coupling_mask[0],
        coupling[0],
        *stacks,
        out_specs=[vmem()] * (len(stacks) + 4),
        scratch=[pltpu.VMEM((3, *square), F32), pltpu.SemaphoreType.DMA((len(stacks),))],
    )
    counts = [3 * rows // 4, rows // 4] if rows % 32 == 0 else [rows]
    parts = call(
        functools.partial(turn_kernel, groups, counts),
        [shape(count, e_dev, orbitals) for count in counts for _ in range(groups)],
        [smem, hbm],
        me,
        great,
        out_specs=[vmem()] * (groups * len(counts)),
        scratch=[
            pltpu.VMEM((e_dev, orbitals, orbitals), BF16),
            pltpu.VMEM((orbitals * e_dev, orbitals), F32),
            pltpu.SemaphoreType.DMA((4,)),
        ],
    )
    great = [exchange(parts[:groups])]
    if len(counts) > 1:
        held = lax.optimization_barrier((*parts[groups:], *less, fwd_e))
        great.append(exchange(held[:groups]))
        less, fwd_e = held[groups:-1], held[-1]
    less = call(
        spectrum_kernel,
        shape(rows // WIDE, fwd_e.shape[0], WIDE * orbitals, dtype=F32),
        [vmem()] * (1 + groups),
        fwd_e,
        *less,
        out_specs=vmem(),
        scratch=[pltpu.VMEM((total * rows, orbitals), F32)],
    )
    pol = []
    for c, count in enumerate(counts):
        last = c == len(counts) - 1
        outs = (
            [shape(lags, rows, orbitals)] * (halves * groups)
            if last
            else [shape(total, count, orbitals)]
        )
        pol += call(
            functools.partial(pol_kernel, groups, halves, sum(counts[:c]), c),
            outs,
            [vmem()] * (3 + groups + c),
            fwd_e,
            back_l,
            less,
            *great[c],
            *pol,
            out_specs=[vmem()] * len(outs),
            scratch=[pltpu.VMEM((total * count, orbitals), F32)],
        )
    pol = pol[len(counts) - 1 :]
    pol = [exchange(pol[h * groups : (h + 1) * groups]) for h in range(halves)]

    near_pairs = [(b, b ^ 1) for b in range(peers) if b ^ 1 < peers]
    far_pairs = [(b, ((b + 1) ^ 1) - 1) for b in range(1, peers) if ((b + 1) ^ 1) - 1 < peers]
    inter = []
    for h in range(halves):
        own = call(
            assemble_kernel,
            shape(lags, orbitals, orbitals),
            [vmem()] * groups,
            *pol[h],
            out_specs=vmem(),
        )
        far = lax.ppermute(own, "block", far_pairs)
        near = lax.ppermute(own, "block", near_pairs)
        partial = call(
            near_kernel,
            shape(lags, orbitals, orbitals, dtype=F32),
            [vmem()] * 4,
            near_left,
            near_right,
            own,
            near,
            out_specs=vmem(),
        )
        parts = call(
            functools.partial(far_kernel, groups),
            [shape(rows, lags, orbitals)] * groups,
            [smem] + [vmem()] * 4,
            me,
            far_left,
            far_right,
            partial,
            far,
            out_specs=[vmem()] * groups,
            scratch=[pltpu.VMEM((orbitals * lags, orbitals), F32)],
        )
        inter += exchange(parts)

    sigma = call(
        functools.partial(sigma_kernel, groups, halves),
        [shape(rows, e_dev, orbitals)] * groups,
        [vmem()] * (3 + groups * halves),
        fwd_l,
        back_e,
        less,
        *inter,
        out_specs=[vmem()] * groups,
    )
    sigma = exchange(sigma)
    out = []
    for which in (list(range(groups // 2)), list(range(groups // 2, groups))):
        out = [
            call(
                functools.partial(final_kernel, groups, which),
                shape(e_dev, orbitals, orbitals, dtype=F32),
                [smem] + [vmem()] * len(which) + [hbm] * len(out),
                me,
                *[sigma[d] for d in which],
                *out,
                out_specs=hbm,
                scratch=[
                    pltpu.VMEM((len(which), e_dev * rows, orbitals), F32),
                    pltpu.SemaphoreType.DMA((len(which),)),
                ],
                input_output_aliases={1 + len(which): 0} if out else {},
            )
        ]
    return out[0].reshape(e_dev, 1, orbitals, orbitals)


def solution(mesh):
    return jax.shard_map(
        shards,
        mesh=mesh,
        in_specs=(
            P("energy", "block", None, None),
            P("energy", "block", None, None),
            P("block", None, None, None),
            P("block", None),
        ),
        out_specs=P("energy", "block", None, None),
        check_vma=False,
    )
```

```python
import functools
import math

import jax
import jax.numpy as jnp
import numpy as np
from jax import lax
from jax.experimental import pallas as pl
from jax.experimental.pallas import tpu as pltpu
from jax.sharding import PartitionSpec as P

BF16 = jnp.bfloat16
F32 = jnp.float32
WIDE = 8


def split(table):
    upper = table.astype(BF16)
    lower = (table - upper.astype(np.float32)).astype(BF16)
    return upper, lower


def tables(groups, e_dev):
    total = groups * e_dev
    length = 3 * total // 2
    omega = 2.0 * math.pi / length * (np.arange(length // 2) + 0.5)
    scale = 2.0 / (length * math.sqrt(total))
    energies = np.arange(total)
    lags = energies - total // 2

    def forward(points):
        angle = omega[:, None] * points[None, :]
        table = np.concatenate([np.cos(angle), np.sin(angle)], axis=0).astype(np.float32)
        return np.concatenate(split(table), axis=1)

    def backward(points):
        angle = points[:, None] * omega[None, :]
        table = np.concatenate([np.cos(angle), np.sin(angle)], axis=1) * scale
        return np.concatenate(split(table.astype(np.float32)), axis=0)

    def ordered(me):
        return np.concatenate([np.arange(e_dev) + (me ^ d) * e_dev for d in range(groups)])

    fwd_e = np.stack([forward(energies[ordered(me)]) for me in range(groups)])
    fwd_l = np.stack([forward(lags[ordered(me)]) for me in range(groups)])
    back_l = np.stack([backward(lags[ordered(me)]) for me in range(groups)])
    back_e = np.stack([backward(energies[ordered(me)]) for me in range(groups)])
    return fwd_e, fwd_l, back_l, back_e


def params():
    return pltpu.CompilerParams(vmem_limit_bytes=12 * 1024 * 1024)


def vmem():
    return pl.BlockSpec(memory_space=pltpu.VMEM)


def dot(a, b):
    return jnp.dot(a, b, preferred_element_type=F32)


def slice_kernel(groups, me_ref, hbm, *rest):
    outs, sems = rest[:groups], rest[groups]
    rows = outs[0].shape[1]
    copies = []
    for d in range(groups):
        place = pl.ds(pl.multiple_of((me_ref[0] ^ d) * rows, rows), rows)
        copies.append(pltpu.make_async_copy(hbm.at[:, place], outs[d], sems.at[d]))
        copies[d].start()
    for copy in copies:
        copy.wait()


def turn_kernel(groups, counts, me_ref, hbm, *rest):
    outs = rest[: groups * len(counts)]
    x_ref, scratch, sems = rest[groups * len(counts) :]
    e_dev, orbitals, _ = x_ref.shape
    rows = orbitals // groups
    me = me_ref[0]
    span = e_dev // sems.shape[0]
    copies = []
    for p in range(sems.shape[0]):
        part = pl.ds(p * span, span)
        copies.append(pltpu.make_async_copy(hbm.at[part], x_ref.at[part], sems.at[p]))
        copies[p].start()
    for p, copy in enumerate(copies):
        copy.wait()
        for e in range(p * span, (p + 1) * span):
            scratch[pl.ds(e, orbitals, stride=e_dev), :] = x_ref[e].astype(F32).T
    first = 0
    for c, count in enumerate(counts):
        for d in range(groups):
            start = pl.multiple_of(((me ^ d) * rows + first) * e_dev, 8)
            part = scratch[pl.ds(start, count * e_dev), :]
            outs[c * groups + d][...] = part.astype(BF16).reshape(count, e_dev, orbitals)
        first += count


def gathered(refs, i):
    both = jnp.concatenate(
        [jnp.concatenate([ref[i + h] for ref in refs], axis=0) for h in range(WIDE)], axis=1
    )
    return jnp.concatenate([both, both], axis=0)


def inverse(back, spectrum):
    both = dot(back, spectrum.astype(BF16))
    half = both.shape[0] // 2
    return both[:half] + both[half:]


def spectrum_kernel(fwd_ref, *refs):
    less, out, scratch = refs[:-2], refs[-2], refs[-1]
    e_dev, rows, orbitals = less[0].shape
    size = e_dev * rows
    for d, part in enumerate(less):
        scratch[d * size : (d + 1) * size, :] = part[...].astype(F32).reshape(size, orbitals)
    fwd = fwd_ref[...]
    total = e_dev * len(less)
    for n in range(out.shape[0]):
        both = jnp.concatenate(
            [scratch[pl.ds(n * WIDE + h, total, stride=rows), :] for h in range(WIDE)], axis=1
        ).astype(BF16)
        out[n] = dot(fwd, jnp.concatenate([both, both], axis=0))


def pol_kernel(groups, halves, first, earlier, fwd_ref, back_ref, less_ref, *refs):
    great, before = refs[:groups], refs[groups : groups + earlier]
    outs, scratch = refs[groups + earlier : -1], refs[-1]
    count, e_dev, orbitals = great[0].shape
    freq = fwd_ref.shape[0] // 2
    fwd, back = fwd_ref[...], back_ref[...]
    total = groups * e_dev
    for i in range(0, count, WIDE):
        a = less_ref[(first + i) // WIDE]
        b = dot(fwd, gathered(great, i))
        real = a[:freq] * b[:freq] + a[freq:] * b[freq:]
        imag = a[freq:] * b[:freq] - a[:freq] * b[freq:]
        pol = inverse(back, jnp.concatenate([real, imag], axis=0))
        for h in range(WIDE):
            scratch[pl.ds(i + h, total, stride=count), :] = pol[
                :, h * orbitals : (h + 1) * orbitals
            ]
    if len(outs) == 1:
        outs[0][...] = scratch[...].astype(BF16).reshape(total, count, orbitals)
        return
    lags = e_dev // halves
    for h in range(halves):
        for d in range(groups):
            out = outs[h * groups + d]
            start = d * e_dev + h * lags
            at = 0
            for ref in before:
                out[:, at : at + ref.shape[1], :] = ref[start : start + lags]
                at += ref.shape[1]
            out[:, first:, :] = (
                scratch[start * count : (start + lags) * count, :]
                .astype(BF16)
                .reshape(lags, count, orbitals)
            )


def sigma_kernel(groups, first, offsets, fwd_l_ref, back_ref, less_ref, *refs):
    halves = len(offsets)
    inter, outs = refs[: groups * halves], refs[groups * halves :]
    count, e_dev, orbitals = outs[0].shape
    freq = fwd_l_ref.shape[0] // 2
    fwd_l, back = fwd_l_ref[...], back_ref[...]
    inter = [
        inter[h * groups + d].at[offsets[h] : offsets[h] + count]
        for d in range(groups)
        for h in range(halves)
    ]
    for i in range(0, count, WIDE):
        a = less_ref[(first + i) // WIDE]
        b = dot(fwd_l, gathered(inter, i))
        real = a[:freq] * b[:freq] - a[freq:] * b[freq:]
        imag = a[freq:] * b[:freq] + a[:freq] * b[freq:]
        sigma = inverse(back, jnp.concatenate([real, imag], axis=0)).astype(BF16)
        for h in range(WIDE):
            for d in range(groups):
                outs[d][i + h] = sigma[
                    d * e_dev : (d + 1) * e_dev, h * orbitals : (h + 1) * orbitals
                ]


def assemble_kernel(*refs):
    ins, out = refs[:-1], refs[-1]
    at = 0
    for part in ins:
        out[:, at : at + part.shape[1], :] = part[...]
        at += part.shape[1]


def diagonal(a, b):
    zero = jnp.zeros_like(a)
    return jnp.concatenate(
        [jnp.concatenate([a, zero], axis=1), jnp.concatenate([zero, b], axis=1)], axis=0
    )


def setup_kernel(groups, count, me_ref, odd_ref, mask_ref, v_ref, *refs):
    sources, outs = refs[:count], refs[count : 2 * count]
    near_left, near_right, far_left, far_right, scratch, sems = refs[2 * count :]
    me = me_ref[0]
    copies = [
        pltpu.make_async_copy(src.at[me], dst, sems.at[n])
        for n, (src, dst) in enumerate(zip(sources, outs))
    ]
    for copy in copies:
        copy.start()
    odd = odd_ref[0]
    scratch[0] = v_ref[1].astype(F32).T
    scratch[1] = v_ref[2 - 2 * odd].astype(F32).T
    scratch[2] = v_ref[2 * odd].astype(F32).T
    rows = scratch.shape[1] // groups

    def ordered(n):
        parts = [
            scratch[n, pl.ds(pl.multiple_of((me ^ d) * rows, rows), rows), :] for d in range(groups)
        ]
        return jnp.concatenate(parts, axis=0).T.astype(BF16)

    def masked(n, t):
        return (scratch[n] * mask_ref[t].astype(F32)).astype(BF16)

    near_left[...] = jnp.concatenate([ordered(0), ordered(1)], axis=1)
    near_right[...] = diagonal(scratch[0].astype(BF16), masked(1, 1 - odd))
    far_left[...] = ordered(2)
    far_right[...] = masked(2, odd)
    for copy in copies:
        copy.wait()


def near_kernel(left, right, own, near, out):
    lags, n, _ = own.shape
    both = jnp.concatenate([own[...].reshape(lags * n, n), near[...].reshape(lags * n, n)], axis=1)
    half = dot(both, right[...]).astype(BF16)
    half = jnp.concatenate(
        [
            jnp.concatenate([half[k * n : k * n + n, :n], half[k * n : k * n + n, n:]], axis=0)
            for k in range(lags)
        ],
        axis=1,
    )
    terms = dot(left[...], half)
    for k in range(lags):
        out[k] = terms[:, k * n : k * n + n]


def far_kernel(groups, me_ref, left, right, partial, far, *refs):
    outs, scratch = refs[:-1], refs[-1]
    lags, n, _ = partial.shape
    rows = n // groups
    me = me_ref[0]
    half = dot(far[...].reshape(lags * n, n), right[...]).astype(BF16)
    half = jnp.concatenate([half[k * n : k * n + n] for k in range(lags)], axis=1)
    terms = dot(left[...], half)
    for k in range(lags):
        scratch[pl.ds(k, n, stride=lags), :] = partial[k] + terms[:, k * n : k * n + n]
    first = 0
    for c in range(0, len(outs), groups):
        count = outs[c].shape[0]
        for d in range(groups):
            start = pl.multiple_of(((me ^ d) * rows + first) * lags, 8)
            part = scratch[pl.ds(start, count * lags), :]
            outs[c + d][...] = part.astype(BF16).reshape(count, lags, n)
        first += count


def final_kernel(groups, first, me_ref, *refs):
    ins, out, scratch, sems = refs[:groups], refs[-3], refs[-2], refs[-1]
    count, e_dev, orbitals = ins[0].shape
    rows = orbitals // groups
    me = me_ref[0]
    copies = []
    for d in range(groups):
        for i in range(count):
            scratch[d, pl.ds(i, e_dev, stride=count), :] = ins[d][i].astype(F32)
        start = pl.multiple_of((me ^ d) * rows + first, 8)
        copies.append(
            pltpu.make_async_copy(
                scratch.at[d].reshape(e_dev, count, orbitals),
                out.at[:, pl.ds(start, count), :],
                sems.at[d],
            )
        )
        copies[-1].start()
    for copy in copies:
        copy.wait()


def exchange(parts):
    groups = lax.axis_size("energy")
    moved = [parts[0]]
    for d in range(1, groups):
        moved.append(lax.ppermute(parts[d], "energy", [(i, i ^ d) for i in range(groups)]))
    return moved


def call(kernel, out_shape, specs, *args, scratch=(), **kwargs):
    return pl.pallas_call(
        kernel,
        out_shape=out_shape,
        in_specs=specs,
        scratch_shapes=list(scratch),
        compiler_params=params(),
        **kwargs,
    )(*args)


def shards(g_less, g_great, coupling, coupling_mask):
    e_dev, _, orbitals, _ = g_less.shape
    groups = lax.axis_size("energy")
    peers = lax.axis_size("block")
    rows = orbitals // groups
    total = e_dev * groups
    halves = 2 if e_dev % 32 == 0 else 1
    lags = e_dev // halves
    index = lax.axis_index("energy")
    me = index.astype(jnp.int32)[None]
    odd = (lax.axis_index("block") % 2).astype(jnp.int32)[None]
    smem = pl.BlockSpec(memory_space=pltpu.SMEM)
    hbm = pl.BlockSpec(memory_space=pltpu.HBM)

    def shape(*dims, dtype=BF16):
        return jax.ShapeDtypeStruct(dims, dtype)

    less = g_less.reshape(e_dev, orbitals, orbitals)
    great = g_great.reshape(e_dev, orbitals, orbitals)
    less, great = [pltpu.with_memory_space_constraint(x, pltpu.HBM) for x in (less, great)]

    parts = [shape(e_dev, rows, orbitals)] * groups
    less = call(
        functools.partial(slice_kernel, groups),
        parts,
        [smem, hbm],
        me,
        less,
        out_specs=[vmem()] * groups,
        scratch=[pltpu.SemaphoreType.DMA((groups,))],
    )
    less = exchange(less)
    stacks = [pltpu.with_memory_space_constraint(jnp.asarray(t), pltpu.HBM) for t in tables(groups, e_dev)]
    square = (orbitals, orbitals)
    fwd_e, fwd_l, back_l, back_e, near_left, near_right, far_left, far_right = call(
        functools.partial(setup_kernel, groups, len(stacks)),
        [shape(*t.shape[1:]) for t in stacks]
        + [shape(orbitals, 2 * orbitals), shape(2 * orbitals, 2 * orbitals)]
        + [shape(*square), shape(*square)],
        [smem, smem, smem, vmem()] + [hbm] * len(stacks),
        me,
        odd,
        coupling_mask[0],
        coupling[0],
        *stacks,
        out_specs=[vmem()] * (len(stacks) + 4),
        scratch=[pltpu.VMEM((3, *square), F32), pltpu.SemaphoreType.DMA((len(stacks),))],
    )
    counts = [3 * rows // 4, rows // 4] if rows % 32 == 0 else [rows]
    parts = call(
        functools.partial(turn_kernel, groups, counts),
        [shape(count, e_dev, orbitals) for count in counts for _ in range(groups)],
        [smem, hbm],
        me,
        great,
        out_specs=[vmem()] * (groups * len(counts)),
        scratch=[
            pltpu.VMEM((e_dev, orbitals, orbitals), BF16),
            pltpu.VMEM((orbitals * e_dev, orbitals), F32),
            pltpu.SemaphoreType.DMA((4,)),
        ],
    )
    great = [exchange(parts[:groups])]
    if len(counts) > 1:
        held = lax.optimization_barrier((*parts[groups:], *less, fwd_e))
        great.append(exchange(held[:groups]))
        less, fwd_e = held[groups:-1], held[-1]
    less = call(
        spectrum_kernel,
        shape(rows // WIDE, fwd_e.shape[0], WIDE * orbitals, dtype=F32),
        [vmem()] * (1 + groups),
        fwd_e,
        *less,
        out_specs=vmem(),
        scratch=[pltpu.VMEM((total * rows, orbitals), F32)],
    )
    pol = []
    for c, count in enumerate(counts):
        last = c == len(counts) - 1
        outs = (
            [shape(lags, rows, orbitals)] * (halves * groups)
            if last
            else [shape(total, count, orbitals)]
        )
        pol += call(
            functools.partial(pol_kernel, groups, halves, sum(counts[:c]), c),
            outs,
            [vmem()] * (3 + groups + c),
            fwd_e,
            back_l,
            less,
            *great[c],
            *pol,
            out_specs=[vmem()] * len(outs),
            scratch=[pltpu.VMEM((total * count, orbitals), F32)],
        )
    pol = pol[len(counts) - 1 :]
    pol = [exchange(pol[h * groups : (h + 1) * groups]) for h in range(halves)]

    near_pairs = [(b, b ^ 1) for b in range(peers) if b ^ 1 < peers]
    far_pairs = [(b, ((b + 1) ^ 1) - 1) for b in range(1, peers) if ((b + 1) ^ 1) - 1 < peers]
    inter = []
    for h in range(halves):
        parts = pol[h]
        own = call(
            assemble_kernel,
            shape(lags, orbitals, orbitals),
            [vmem()] * len(parts),
            *parts,
            out_specs=vmem(),
        )
        far = lax.ppermute(own, "block", far_pairs)
        near = lax.ppermute(own, "block", near_pairs)
        partial = call(
            near_kernel,
            shape(lags, orbitals, orbitals, dtype=F32),
            [vmem()] * 4,
            near_left,
            near_right,
            own,
            near,
            out_specs=vmem(),
        )
        cut = [rows]
        parts = call(
            functools.partial(far_kernel, groups),
            [shape(count, lags, orbitals) for count in cut for _ in range(groups)],
            [smem] + [vmem()] * 4,
            me,
            far_left,
            far_right,
            partial,
            far,
            out_specs=[vmem()] * (groups * len(cut)),
            scratch=[pltpu.VMEM((orbitals * lags, orbitals), F32)],
        )
        inter.append(
            [exchange(parts[c * groups : (c + 1) * groups]) for c in range(len(cut))]
        )

    sigma = []
    for c, count in enumerate(counts):
        first = sum(counts[:c])
        parts = call(
            functools.partial(sigma_kernel, groups, first, [first] * halves),
            [shape(count, e_dev, orbitals)] * groups,
            [vmem()] * (3 + groups * halves),
            fwd_l,
            back_e,
            less,
            *[part for half in inter for part in half[0]],
            out_specs=[vmem()] * groups,
        )
        sigma.append((first, count, exchange(parts)))
    out = []
    for first, count, parts in sigma:
        out = [
            call(
                functools.partial(final_kernel, groups, first),
                shape(e_dev, orbitals, orbitals, dtype=F32),
                [smem] + [vmem()] * groups + [hbm] * len(out),
                me,
                *parts,
                *out,
                out_specs=hbm,
                scratch=[
                    pltpu.VMEM((groups, e_dev * count, orbitals), F32),
                    pltpu.SemaphoreType.DMA((groups,)),
                ],
                input_output_aliases={1 + groups: 0} if out else {},
            )
        ]
    return out[0].reshape(e_dev, 1, orbitals, orbitals)


def solution(mesh):
    return jax.shard_map(
        shards,
        mesh=mesh,
        in_specs=(
            P("energy", "block", None, None),
            P("energy", "block", None, None),
            P("block", None, None, None),
            P("block", None),
        ),
        out_specs=P("energy", "block", None, None),
        check_vma=False,
    )
```

```python
import functools
import math

import jax
import jax.numpy as jnp
import numpy as np
from jax import lax
from jax.experimental import pallas as pl
from jax.experimental.pallas import tpu as pltpu
from jax.sharding import PartitionSpec as P

BF16 = jnp.bfloat16
F32 = jnp.float32
WIDE = 8


def split(table):
    upper = table.astype(BF16)
    lower = (table - upper.astype(np.float32)).astype(BF16)
    return upper, lower


def tables(groups, e_dev):
    total = groups * e_dev
    length = 3 * total // 2
    omega = 2.0 * math.pi / length * (np.arange(length // 2) + 0.5)
    scale = 2.0 / (length * math.sqrt(total))
    energies = np.arange(total)
    lags = energies - total // 2

    def forward(points):
        angle = omega[:, None] * points[None, :]
        table = np.concatenate([np.cos(angle), np.sin(angle)], axis=0).astype(np.float32)
        return np.concatenate(split(table), axis=1)

    def backward(points):
        angle = points[:, None] * omega[None, :]
        table = np.concatenate([np.cos(angle), np.sin(angle)], axis=1) * scale
        return np.concatenate(split(table.astype(np.float32)), axis=0)

    def ordered(me):
        return np.concatenate([np.arange(e_dev) + (me ^ d) * e_dev for d in range(groups)])

    fwd_e = np.stack([forward(energies[ordered(me)]) for me in range(groups)])
    fwd_l = np.stack([forward(lags[ordered(me)]) for me in range(groups)])
    back_l = np.stack([backward(lags[ordered(me)]) for me in range(groups)])
    back_e = np.stack([backward(energies[ordered(me)]) for me in range(groups)])
    return fwd_e, fwd_l, back_l, back_e


def params():
    return pltpu.CompilerParams(vmem_limit_bytes=12 * 1024 * 1024)


def vmem():
    return pl.BlockSpec(memory_space=pltpu.VMEM)


def dot(a, b):
    return jnp.dot(a, b, preferred_element_type=F32)


def slice_kernel(groups, me_ref, hbm, *rest):
    outs, sems = rest[:groups], rest[groups]
    rows = outs[0].shape[1]
    copies = []
    for d in range(groups):
        place = pl.ds(pl.multiple_of((me_ref[0] ^ d) * rows, rows), rows)
        copies.append(pltpu.make_async_copy(hbm.at[:, place], outs[d], sems.at[d]))
        copies[d].start()
    for copy in copies:
        copy.wait()


def turn_kernel(groups, counts, me_ref, hbm, *rest):
    outs = rest[: groups * len(counts)]
    x_ref, scratch, sems = rest[groups * len(counts) :]
    e_dev, orbitals, _ = x_ref.shape
    rows = orbitals // groups
    me = me_ref[0]
    span = e_dev // sems.shape[0]
    copies = []
    for p in range(sems.shape[0]):
        part = pl.ds(p * span, span)
        copies.append(pltpu.make_async_copy(hbm.at[part], x_ref.at[part], sems.at[p]))
        copies[p].start()
    for p, copy in enumerate(copies):
        copy.wait()
        for e in range(p * span, (p + 1) * span):
            scratch[pl.ds(e, orbitals, stride=e_dev), :] = x_ref[e].astype(F32).T
    first = 0
    for c, count in enumerate(counts):
        for d in range(groups):
            start = pl.multiple_of(((me ^ d) * rows + first) * e_dev, 8)
            part = scratch[pl.ds(start, count * e_dev), :]
            outs[c * groups + d][...] = part.astype(BF16).reshape(count, e_dev, orbitals)
        first += count


def gathered(refs, i):
    both = jnp.concatenate(
        [jnp.concatenate([ref[i + h] for ref in refs], axis=0) for h in range(WIDE)], axis=1
    )
    return jnp.concatenate([both, both], axis=0)


def inverse(back, spectrum):
    both = dot(back, spectrum.astype(BF16))
    half = both.shape[0] // 2
    return both[:half] + both[half:]


def spectrum_kernel(fwd_ref, *refs):
    less, out, scratch = refs[:-2], refs[-2], refs[-1]
    e_dev, rows, orbitals = less[0].shape
    size = e_dev * rows
    for d, part in enumerate(less):
        scratch[d * size : (d + 1) * size, :] = part[...].astype(F32).reshape(size, orbitals)
    fwd = fwd_ref[...]
    total = e_dev * len(less)
    for n in range(out.shape[0]):
        both = jnp.concatenate(
            [scratch[pl.ds(n * WIDE + h, total, stride=rows), :] for h in range(WIDE)], axis=1
        ).astype(BF16)
        out[n] = dot(fwd, jnp.concatenate([both, both], axis=0))


def pol_kernel(groups, halves, first, earlier, fwd_ref, back_ref, less_ref, *refs):
    great, before = refs[:groups], refs[groups : groups + earlier]
    outs, scratch = refs[groups + earlier : -1], refs[-1]
    count, e_dev, orbitals = great[0].shape
    freq = fwd_ref.shape[0] // 2
    fwd, back = fwd_ref[...], back_ref[...]
    total = groups * e_dev
    for i in range(0, count, WIDE):
        a = less_ref[(first + i) // WIDE]
        b = dot(fwd, gathered(great, i))
        real = a[:freq] * b[:freq] + a[freq:] * b[freq:]
        imag = a[freq:] * b[:freq] - a[:freq] * b[freq:]
        pol = inverse(back, jnp.concatenate([real, imag], axis=0))
        for h in range(WIDE):
            scratch[pl.ds(i + h, total, stride=count), :] = pol[
                :, h * orbitals : (h + 1) * orbitals
            ]
    lags = e_dev // halves

    def part(d, h):
        start = (d * halves + h) * lags * count
        return scratch[start : start + lags * count, :].astype(BF16).reshape(lags, count, orbitals)

    for d in range(groups):
        outs[d][...] = part(d, 0)
        for h in range(1, halves):
            out = outs[h * groups + d]
            at = 0
            for ref in before[(h - 1) * groups + d :: (halves - 1) * groups]:
                out[:, at : at + ref.shape[1], :] = ref[...]
                at += ref.shape[1]
            out[:, at:, :] = part(d, h)


def sigma_kernel(groups, first, offsets, fwd_l_ref, back_ref, less_ref, *refs):
    halves = len(offsets)
    inter, outs = refs[: groups * halves], refs[groups * halves :]
    count, e_dev, orbitals = outs[0].shape
    freq = fwd_l_ref.shape[0] // 2
    fwd_l, back = fwd_l_ref[...], back_ref[...]
    inter = [
        inter[h * groups + d].at[offsets[h] : offsets[h] + count]
        for d in range(groups)
        for h in range(halves)
    ]
    for i in range(0, count, WIDE):
        a = less_ref[(first + i) // WIDE]
        b = dot(fwd_l, gathered(inter, i))
        real = a[:freq] * b[:freq] - a[freq:] * b[freq:]
        imag = a[freq:] * b[:freq] + a[:freq] * b[freq:]
        sigma = inverse(back, jnp.concatenate([real, imag], axis=0)).astype(BF16)
        for h in range(WIDE):
            for d in range(groups):
                outs[d][i + h] = sigma[
                    d * e_dev : (d + 1) * e_dev, h * orbitals : (h + 1) * orbitals
                ]


def assemble_kernel(*refs):
    ins, out = refs[:-1], refs[-1]
    at = 0
    for part in ins:
        out[:, at : at + part.shape[1], :] = part[...]
        at += part.shape[1]


def diagonal(a, b):
    zero = jnp.zeros_like(a)
    return jnp.concatenate(
        [jnp.concatenate([a, zero], axis=1), jnp.concatenate([zero, b], axis=1)], axis=0
    )


def setup_kernel(groups, count, me_ref, odd_ref, mask_ref, v_ref, *refs):
    sources, outs = refs[:count], refs[count : 2 * count]
    near_left, near_right, far_left, far_right, scratch, sems = refs[2 * count :]
    me = me_ref[0]
    copies = [
        pltpu.make_async_copy(src.at[me], dst, sems.at[n])
        for n, (src, dst) in enumerate(zip(sources, outs))
    ]
    for copy in copies:
        copy.start()
    odd = odd_ref[0]
    scratch[0] = v_ref[1].astype(F32).T
    scratch[1] = v_ref[2 - 2 * odd].astype(F32).T
    scratch[2] = v_ref[2 * odd].astype(F32).T
    rows = scratch.shape[1] // groups

    def ordered(n):
        parts = [
            scratch[n, pl.ds(pl.multiple_of((me ^ d) * rows, rows), rows), :] for d in range(groups)
        ]
        return jnp.concatenate(parts, axis=0).T.astype(BF16)

    def masked(n, t):
        return (scratch[n] * mask_ref[t].astype(F32)).astype(BF16)

    near_left[...] = jnp.concatenate([ordered(0), ordered(1)], axis=1)
    near_right[...] = diagonal(scratch[0].astype(BF16), masked(1, 1 - odd))
    far_left[...] = ordered(2)
    far_right[...] = masked(2, odd)
    for copy in copies:
        copy.wait()


def near_kernel(left, right, own, near, out):
    lags, n, _ = own.shape
    both = jnp.concatenate([own[...].reshape(lags * n, n), near[...].reshape(lags * n, n)], axis=1)
    half = dot(both, right[...]).astype(BF16)
    half = jnp.concatenate(
        [
            jnp.concatenate([half[k * n : k * n + n, :n], half[k * n : k * n + n, n:]], axis=0)
            for k in range(lags)
        ],
        axis=1,
    )
    terms = dot(left[...], half)
    for k in range(lags):
        out[k] = terms[:, k * n : k * n + n]


def far_kernel(groups, me_ref, left, right, partial, far, *refs):
    outs, scratch = refs[:-1], refs[-1]
    lags, n, _ = partial.shape
    rows = n // groups
    me = me_ref[0]
    half = dot(far[...].reshape(lags * n, n), right[...]).astype(BF16)
    half = jnp.concatenate([half[k * n : k * n + n] for k in range(lags)], axis=1)
    terms = dot(left[...], half)
    for k in range(lags):
        scratch[pl.ds(k, n, stride=lags), :] = partial[k] + terms[:, k * n : k * n + n]
    first = 0
    for c in range(0, len(outs), groups):
        count = outs[c].shape[0]
        for d in range(groups):
            start = pl.multiple_of(((me ^ d) * rows + first) * lags, 8)
            part = scratch[pl.ds(start, count * lags), :]
            outs[c + d][...] = part.astype(BF16).reshape(count, lags, n)
        first += count


def final_kernel(groups, first, me_ref, *refs):
    ins, out, scratch, sems = refs[:groups], refs[-3], refs[-2], refs[-1]
    count, e_dev, orbitals = ins[0].shape
    rows = orbitals // groups
    me = me_ref[0]
    copies = []
    for d in range(groups):
        for i in range(count):
            scratch[d, pl.ds(i, e_dev, stride=count), :] = ins[d][i].astype(F32)
        start = pl.multiple_of((me ^ d) * rows + first, 8)
        copies.append(
            pltpu.make_async_copy(
                scratch.at[d].reshape(e_dev, count, orbitals),
                out.at[:, pl.ds(start, count), :],
                sems.at[d],
            )
        )
        copies[-1].start()
    for copy in copies:
        copy.wait()


def exchange(parts):
    groups = lax.axis_size("energy")
    moved = [parts[0]]
    for d in range(1, groups):
        moved.append(lax.ppermute(parts[d], "energy", [(i, i ^ d) for i in range(groups)]))
    return moved


def call(kernel, out_shape, specs, *args, scratch=(), **kwargs):
    return pl.pallas_call(
        kernel,
        out_shape=out_shape,
        in_specs=specs,
        scratch_shapes=list(scratch),
        compiler_params=params(),
        **kwargs,
    )(*args)


def shards(g_less, g_great, coupling, coupling_mask):
    e_dev, _, orbitals, _ = g_less.shape
    groups = lax.axis_size("energy")
    peers = lax.axis_size("block")
    rows = orbitals // groups
    total = e_dev * groups
    halves = 2 if e_dev % 32 == 0 else 1
    lags = e_dev // halves
    index = lax.axis_index("energy")
    me = index.astype(jnp.int32)[None]
    odd = (lax.axis_index("block") % 2).astype(jnp.int32)[None]
    smem = pl.BlockSpec(memory_space=pltpu.SMEM)
    hbm = pl.BlockSpec(memory_space=pltpu.HBM)

    def shape(*dims, dtype=BF16):
        return jax.ShapeDtypeStruct(dims, dtype)

    less = g_less.reshape(e_dev, orbitals, orbitals)
    great = g_great.reshape(e_dev, orbitals, orbitals)
    less, great = [pltpu.with_memory_space_constraint(x, pltpu.HBM) for x in (less, great)]

    parts = [shape(e_dev, rows, orbitals)] * groups
    less = call(
        functools.partial(slice_kernel, groups),
        parts,
        [smem, hbm],
        me,
        less,
        out_specs=[vmem()] * groups,
        scratch=[pltpu.SemaphoreType.DMA((groups,))],
    )
    less = exchange(less)
    stacks = [pltpu.with_memory_space_constraint(jnp.asarray(t), pltpu.HBM) for t in tables(groups, e_dev)]
    square = (orbitals, orbitals)
    fwd_e, fwd_l, back_l, back_e, near_left, near_right, far_left, far_right = call(
        functools.partial(setup_kernel, groups, len(stacks)),
        [shape(*t.shape[1:]) for t in stacks]
        + [shape(orbitals, 2 * orbitals), shape(2 * orbitals, 2 * orbitals)]
        + [shape(*square), shape(*square)],
        [smem, smem, smem, vmem()] + [hbm] * len(stacks),
        me,
        odd,
        coupling_mask[0],
        coupling[0],
        *stacks,
        out_specs=[vmem()] * (len(stacks) + 4),
        scratch=[pltpu.VMEM((3, *square), F32), pltpu.SemaphoreType.DMA((len(stacks),))],
    )
    counts = [rows // 2, rows // 2] if rows % 32 == 0 else [rows]
    parts = call(
        functools.partial(turn_kernel, groups, counts),
        [shape(count, e_dev, orbitals) for count in counts for _ in range(groups)],
        [smem, hbm],
        me,
        great,
        out_specs=[vmem()] * (groups * len(counts)),
        scratch=[
            pltpu.VMEM((e_dev, orbitals, orbitals), BF16),
            pltpu.VMEM((orbitals * e_dev, orbitals), F32),
            pltpu.SemaphoreType.DMA((4,)),
        ],
    )
    great = [exchange(parts[:groups])]
    rest = parts[groups:]
    less = call(
        spectrum_kernel,
        shape(rows // WIDE, fwd_e.shape[0], WIDE * orbitals, dtype=F32),
        [vmem()] * (1 + groups),
        fwd_e,
        *less,
        out_specs=vmem(),
        scratch=[pltpu.VMEM((total * rows, orbitals), F32)],
    )
    if len(counts) > 1:
        *rest, less = lax.optimization_barrier((*rest, less))
        great.append(exchange(rest))
    pol = [[] for _ in range(halves)]
    later = []
    for c, count in enumerate(counts):
        width = rows if c == len(counts) - 1 else count
        parts = call(
            functools.partial(pol_kernel, groups, halves, sum(counts[:c]), len(later)),
            [shape(lags, count, orbitals)] * groups
            + [shape(lags, width, orbitals)] * ((halves - 1) * groups),
            [vmem()] * (3 + groups + len(later)),
            fwd_e,
            back_l,
            less,
            *great[c],
            *later,
            out_specs=[vmem()] * (halves * groups),
            scratch=[pltpu.VMEM((total * count, orbitals), F32)],
        )
        pol[0].append(exchange(parts[:groups]))
        later += parts[groups:]
    for h in range(1, halves):
        last = len(later) - (halves - h) * groups
        pol[h].append(exchange(later[last : last + groups]))

    near_pairs = [(b, b ^ 1) for b in range(peers) if b ^ 1 < peers]
    far_pairs = [(b, ((b + 1) ^ 1) - 1) for b in range(1, peers) if ((b + 1) ^ 1) - 1 < peers]
    inter = []
    for h in range(halves):
        parts = [chunk[d] for d in range(groups) for chunk in pol[h]]
        own = call(
            assemble_kernel,
            shape(lags, orbitals, orbitals),
            [vmem()] * len(parts),
            *parts,
            out_specs=vmem(),
        )
        far = lax.ppermute(own, "block", far_pairs)
        near = lax.ppermute(own, "block", near_pairs)
        partial = call(
            near_kernel,
            shape(lags, orbitals, orbitals, dtype=F32),
            [vmem()] * 4,
            near_left,
            near_right,
            own,
            near,
            out_specs=vmem(),
        )
        cut = [rows]
        parts = call(
            functools.partial(far_kernel, groups),
            [shape(count, lags, orbitals) for count in cut for _ in range(groups)],
            [smem] + [vmem()] * 4,
            me,
            far_left,
            far_right,
            partial,
            far,
            out_specs=[vmem()] * (groups * len(cut)),
            scratch=[pltpu.VMEM((orbitals * lags, orbitals), F32)],
        )
        inter.append(
            [exchange(parts[c * groups : (c + 1) * groups]) for c in range(len(cut))]
        )

    counts = [3 * rows // 4, rows // 4] if rows % 32 == 0 else [rows]
    sigma = []
    for c, count in enumerate(counts):
        first = sum(counts[:c])
        parts = call(
            functools.partial(sigma_kernel, groups, first, [first] * halves),
            [shape(count, e_dev, orbitals)] * groups,
            [vmem()] * (3 + groups * halves),
            fwd_l,
            back_e,
            less,
            *[part for half in inter for part in half[0]],
            out_specs=[vmem()] * groups,
        )
        sigma.append((first, count, exchange(parts)))
    out = []
    for first, count, parts in sigma:
        out = [
            call(
                functools.partial(final_kernel, groups, first),
                shape(e_dev, orbitals, orbitals, dtype=F32),
                [smem] + [vmem()] * groups + [hbm] * len(out),
                me,
                *parts,
                *out,
                out_specs=hbm,
                scratch=[
                    pltpu.VMEM((groups, e_dev * count, orbitals), F32),
                    pltpu.SemaphoreType.DMA((groups,)),
                ],
                input_output_aliases={1 + groups: 0} if out else {},
            )
        ]
    return out[0].reshape(e_dev, 1, orbitals, orbitals)


def solution(mesh):
    return jax.shard_map(
        shards,
        mesh=mesh,
        in_specs=(
            P("energy", "block", None, None),
            P("energy", "block", None, None),
            P("block", None, None, None),
            P("block", None),
        ),
        out_specs=P("energy", "block", None, None),
        check_vma=False,
    )
```

```python
import functools
import math

import jax
import jax.numpy as jnp
import numpy as np
from jax import lax
from jax.experimental import pallas as pl
from jax.experimental.pallas import tpu as pltpu
from jax.sharding import PartitionSpec as P

BF16 = jnp.bfloat16
F32 = jnp.float32


def split(table):
    upper = table.astype(BF16)
    lower = (table - upper.astype(np.float32)).astype(BF16)
    return upper, lower


def tables(groups, e_dev):
    total = groups * e_dev
    length = 3 * total // 2
    omega = 2.0 * math.pi / length * (np.arange(length // 2) + 0.5)
    scale = 2.0 / (length * math.sqrt(total))
    energies = np.arange(total)
    lags = energies - total // 2

    def forward(points):
        angle = omega[:, None] * points[None, :]
        table = np.concatenate([np.cos(angle), np.sin(angle)], axis=0).astype(np.float32)
        return np.concatenate(split(table), axis=1)

    def backward(points):
        angle = points[:, None] * omega[None, :]
        table = np.concatenate([np.cos(angle), np.sin(angle)], axis=1) * scale
        return np.concatenate(split(table.astype(np.float32)), axis=0)

    def ordered(me):
        return np.concatenate([np.arange(e_dev) + (me ^ d) * e_dev for d in range(groups)])

    fwd_e = np.stack([forward(energies[ordered(me)]) for me in range(groups)])
    fwd_l = np.stack([forward(lags[ordered(me)]) for me in range(groups)])
    back_l = np.stack([backward(lags[ordered(me)]) for me in range(groups)])
    back_e = np.stack([backward(energies[ordered(me)]) for me in range(groups)])
    return fwd_e, fwd_l, back_l, back_e


def params():
    return pltpu.CompilerParams(vmem_limit_bytes=12 * 1024 * 1024)


def vmem():
    return pl.BlockSpec(memory_space=pltpu.VMEM)


def dot(a, b):
    return jnp.dot(a, b, preferred_element_type=F32)


def slice_kernel(groups, me_ref, hbm, *rest):
    outs, sems = rest[:groups], rest[groups]
    rows = outs[0].shape[1]
    copies = []
    for d in range(groups):
        place = pl.ds(pl.multiple_of((me_ref[0] ^ d) * rows, rows), rows)
        copies.append(pltpu.make_async_copy(hbm.at[:, place], outs[d], sems.at[d]))
        copies[d].start()
    for copy in copies:
        copy.wait()


def turn_kernel(groups, counts, me_ref, hbm, *rest):
    outs = rest[: groups * len(counts)]
    x_ref, scratch, sems = rest[groups * len(counts) :]
    e_dev, orbitals, _ = x_ref.shape
    rows = orbitals // groups
    me = me_ref[0]
    span = e_dev // sems.shape[0]
    copies = []
    for p in range(sems.shape[0]):
        part = pl.ds(p * span, span)
        copies.append(pltpu.make_async_copy(hbm.at[part], x_ref.at[part], sems.at[p]))
        copies[p].start()
    for p, copy in enumerate(copies):
        copy.wait()
        for e in range(p * span, (p + 1) * span):
            scratch[pl.ds(e, orbitals, stride=e_dev), :] = x_ref[e].astype(F32).T
    first = 0
    for c, count in enumerate(counts):
        for d in range(groups):
            start = pl.multiple_of(((me ^ d) * rows + first) * e_dev, 8)
            part = scratch[pl.ds(start, count * e_dev), :]
            outs[c * groups + d][...] = part.astype(BF16).reshape(count, e_dev, orbitals)
        first += count


def gathered(refs, i, wide):
    both = jnp.concatenate(
        [jnp.concatenate([ref[i + h] for ref in refs], axis=0) for h in range(wide)], axis=1
    )
    return jnp.concatenate([both, both], axis=0)


def inverse(back, spectrum):
    both = dot(back, spectrum.astype(BF16))
    half = both.shape[0] // 2
    return both[:half] + both[half:]


def spectrum_kernel(fwd_ref, *refs):
    less, out, scratch = refs[:-2], refs[-2], refs[-1]
    e_dev, rows, orbitals = less[0].shape
    size = e_dev * rows
    for d, part in enumerate(less):
        scratch[d * size : (d + 1) * size, :] = part[...].astype(F32).reshape(size, orbitals)
    total = e_dev * len(less)
    both = jnp.concatenate(
        [scratch[pl.ds(i, total, stride=rows), :] for i in range(rows)], axis=1
    ).astype(BF16)
    out[...] = dot(fwd_ref[...], jnp.concatenate([both, both], axis=0))


def pol_kernel(groups, halves, first, earlier, fwd_ref, back_ref, less_ref, *refs):
    great, before = refs[:groups], refs[groups : groups + earlier]
    outs, scratch = refs[groups + earlier : -1], refs[-1]
    count, e_dev, orbitals = great[0].shape
    freq = fwd_ref.shape[0] // 2
    fwd, back = fwd_ref[...], back_ref[...]
    total = groups * e_dev
    wide = count
    for i in range(0, count, wide):
        a = less_ref[:, (first + i) * orbitals : (first + i + wide) * orbitals]
        b = dot(fwd, gathered(great, i, wide))
        real = a[:freq] * b[:freq] + a[freq:] * b[freq:]
        imag = a[freq:] * b[:freq] - a[:freq] * b[freq:]
        pol = inverse(back, jnp.concatenate([real, imag], axis=0))
        for h in range(wide):
            scratch[pl.ds(i + h, total, stride=count), :] = pol[
                :, h * orbitals : (h + 1) * orbitals
            ]
    lags = e_dev // halves

    def part(d, h):
        start = (d * halves + h) * lags * count
        return scratch[start : start + lags * count, :].astype(BF16).reshape(lags, count, orbitals)

    for d in range(groups):
        outs[d][...] = part(d, 0)
        for h in range(1, halves):
            out = outs[h * groups + d]
            at = 0
            for ref in before[(h - 1) * groups + d :: (halves - 1) * groups]:
                out[:, at : at + ref.shape[1], :] = ref[...]
                at += ref.shape[1]
            out[:, at:, :] = part(d, h)


def sigma_kernel(groups, first, offsets, fwd_l_ref, back_ref, less_ref, *refs):
    halves = len(offsets)
    inter, outs = refs[: groups * halves], refs[groups * halves :]
    count, e_dev, orbitals = outs[0].shape
    freq = fwd_l_ref.shape[0] // 2
    fwd_l, back = fwd_l_ref[...], back_ref[...]
    inter = [
        inter[h * groups + d].at[offsets[h] : offsets[h] + count]
        for d in range(groups)
        for h in range(halves)
    ]
    wide = count
    for i in range(0, count, wide):
        a = less_ref[:, (first + i) * orbitals : (first + i + wide) * orbitals]
        b = dot(fwd_l, gathered(inter, i, wide))
        real = a[:freq] * b[:freq] - a[freq:] * b[freq:]
        imag = a[freq:] * b[:freq] + a[:freq] * b[freq:]
        sigma = inverse(back, jnp.concatenate([real, imag], axis=0)).astype(BF16)
        for h in range(wide):
            for d in range(groups):
                outs[d][i + h] = sigma[
                    d * e_dev : (d + 1) * e_dev, h * orbitals : (h + 1) * orbitals
                ]


def assemble_kernel(*refs):
    ins, out = refs[:-1], refs[-1]
    at = 0
    for part in ins:
        out[:, at : at + part.shape[1], :] = part[...]
        at += part.shape[1]


def diagonal(a, b):
    zero = jnp.zeros_like(a)
    return jnp.concatenate(
        [jnp.concatenate([a, zero], axis=1), jnp.concatenate([zero, b], axis=1)], axis=0
    )


def setup_kernel(groups, count, me_ref, odd_ref, mask_ref, v_ref, *refs):
    sources, outs = refs[:count], refs[count : 2 * count]
    near_left, near_right, far_left, far_right, scratch, sems = refs[2 * count :]
    me = me_ref[0]
    copies = [
        pltpu.make_async_copy(src.at[me], dst, sems.at[n])
        for n, (src, dst) in enumerate(zip(sources, outs))
    ]
    for copy in copies:
        copy.start()
    odd = odd_ref[0]
    scratch[0] = v_ref[1].astype(F32).T
    scratch[1] = v_ref[2 - 2 * odd].astype(F32).T
    scratch[2] = v_ref[2 * odd].astype(F32).T
    rows = scratch.shape[1] // groups

    def ordered(n):
        parts = [
            scratch[n, pl.ds(pl.multiple_of((me ^ d) * rows, rows), rows), :] for d in range(groups)
        ]
        return jnp.concatenate(parts, axis=0).T.astype(BF16)

    def masked(n, t):
        return (scratch[n] * mask_ref[t].astype(F32)).astype(BF16)

    near_left[...] = jnp.concatenate([ordered(0), ordered(1)], axis=1)
    near_right[...] = diagonal(scratch[0].astype(BF16), masked(1, 1 - odd))
    far_left[...] = ordered(2)
    far_right[...] = masked(2, odd)
    for copy in copies:
        copy.wait()


def near_kernel(left, right, own, near, out):
    lags, n, _ = own.shape
    both = jnp.concatenate([own[...].reshape(lags * n, n), near[...].reshape(lags * n, n)], axis=1)
    half = dot(both, right[...]).astype(BF16)
    half = jnp.concatenate(
        [
            jnp.concatenate([half[k * n : k * n + n, :n], half[k * n : k * n + n, n:]], axis=0)
            for k in range(lags)
        ],
        axis=1,
    )
    terms = dot(left[...], half)
    for k in range(lags):
        out[k] = terms[:, k * n : k * n + n]


def far_kernel(groups, me_ref, left, right, partial, far, *refs):
    outs, scratch = refs[:-1], refs[-1]
    lags, n, _ = partial.shape
    rows = n // groups
    me = me_ref[0]
    half = dot(far[...].reshape(lags * n, n), right[...]).astype(BF16)
    half = jnp.concatenate([half[k * n : k * n + n] for k in range(lags)], axis=1)
    terms = dot(left[...], half)
    for k in range(lags):
        scratch[pl.ds(k, n, stride=lags), :] = partial[k] + terms[:, k * n : k * n + n]
    first = 0
    for c in range(0, len(outs), groups):
        count = outs[c].shape[0]
        for d in range(groups):
            start = pl.multiple_of(((me ^ d) * rows + first) * lags, 8)
            part = scratch[pl.ds(start, count * lags), :]
            outs[c + d][...] = part.astype(BF16).reshape(count, lags, n)
        first += count


def all_kernel(groups, me_ref, near_left, near_right, far_left, far_right, own, near, far, *refs):
    outs, scratch = refs[:-1], refs[-1]
    lags, n, _ = far.shape
    rows = n // groups
    me = me_ref[0]
    both = jnp.concatenate([own[...].reshape(lags * n, n), near[...].reshape(lags * n, n)], axis=1)
    half = dot(both, near_right[...]).astype(BF16)
    other = dot(far[...].reshape(lags * n, n), far_right[...]).astype(BF16)
    half = jnp.concatenate(
        [
            jnp.concatenate(
                [
                    half[k * n : k * n + n, :n],
                    half[k * n : k * n + n, n:],
                    other[k * n : k * n + n],
                ],
                axis=0,
            )
            for k in range(lags)
        ],
        axis=1,
    )
    terms = dot(jnp.concatenate([near_left[...], far_left[...]], axis=1), half)
    for k in range(lags):
        scratch[pl.ds(k, n, stride=lags), :] = terms[:, k * n : k * n + n]
    first = 0
    for c in range(0, len(outs), groups):
        count = outs[c].shape[0]
        for d in range(groups):
            start = pl.multiple_of(((me ^ d) * rows + first) * lags, 8)
            part = scratch[pl.ds(start, count * lags), :]
            outs[c + d][...] = part.astype(BF16).reshape(count, lags, n)
        first += count


def final_kernel(groups, first, me_ref, *refs):
    ins, out, scratch, sems = refs[:groups], refs[-3], refs[-2], refs[-1]
    count, e_dev, orbitals = ins[0].shape
    rows = orbitals // groups
    me = me_ref[0]
    copies = []
    for d in range(groups):
        for i in range(count):
            scratch[d, pl.ds(i, e_dev, stride=count), :] = ins[d][i].astype(F32)
        start = pl.multiple_of((me ^ d) * rows + first, 8)
        copies.append(
            pltpu.make_async_copy(
                scratch.at[d].reshape(e_dev, count, orbitals),
                out.at[:, pl.ds(start, count), :],
                sems.at[d],
            )
        )
        copies[-1].start()
    for copy in copies:
        copy.wait()


def exchange(parts):
    groups = lax.axis_size("energy")
    moved = [parts[0]]
    for d in range(1, groups):
        moved.append(lax.ppermute(parts[d], "energy", [(i, i ^ d) for i in range(groups)]))
    return moved


def call(kernel, out_shape, specs, *args, scratch=(), **kwargs):
    return pl.pallas_call(
        kernel,
        out_shape=out_shape,
        in_specs=specs,
        scratch_shapes=list(scratch),
        compiler_params=params(),
        **kwargs,
    )(*args)


def shards(g_less, g_great, coupling, coupling_mask):
    e_dev, _, orbitals, _ = g_less.shape
    groups = lax.axis_size("energy")
    peers = lax.axis_size("block")
    rows = orbitals // groups
    total = e_dev * groups
    halves = 2 if e_dev % 32 == 0 else 1
    lags = e_dev // halves
    index = lax.axis_index("energy")
    me = index.astype(jnp.int32)[None]
    odd = (lax.axis_index("block") % 2).astype(jnp.int32)[None]
    smem = pl.BlockSpec(memory_space=pltpu.SMEM)
    hbm = pl.BlockSpec(memory_space=pltpu.HBM)

    def shape(*dims, dtype=BF16):
        return jax.ShapeDtypeStruct(dims, dtype)

    less = g_less.reshape(e_dev, orbitals, orbitals)
    great = g_great.reshape(e_dev, orbitals, orbitals)
    less, great = [pltpu.with_memory_space_constraint(x, pltpu.HBM) for x in (less, great)]

    parts = [shape(e_dev, rows, orbitals)] * groups
    less = call(
        functools.partial(slice_kernel, groups),
        parts,
        [smem, hbm],
        me,
        less,
        out_specs=[vmem()] * groups,
        scratch=[pltpu.SemaphoreType.DMA((groups,))],
    )
    less = exchange(less)
    stacks = [pltpu.with_memory_space_constraint(jnp.asarray(t), pltpu.HBM) for t in tables(groups, e_dev)]
    square = (orbitals, orbitals)
    fwd_e, fwd_l, back_l, back_e, near_left, near_right, far_left, far_right = call(
        functools.partial(setup_kernel, groups, len(stacks)),
        [shape(*t.shape[1:]) for t in stacks]
        + [shape(orbitals, 2 * orbitals), shape(2 * orbitals, 2 * orbitals)]
        + [shape(*square), shape(*square)],
        [smem, smem, smem, vmem()] + [hbm] * len(stacks),
        me,
        odd,
        coupling_mask[0],
        coupling[0],
        *stacks,
        out_specs=[vmem()] * (len(stacks) + 4),
        scratch=[pltpu.VMEM((3, *square), F32), pltpu.SemaphoreType.DMA((len(stacks),))],
    )
    counts = [rows // 2, rows // 2] if rows % 32 == 0 else [rows]
    parts = call(
        functools.partial(turn_kernel, groups, counts),
        [shape(count, e_dev, orbitals) for count in counts for _ in range(groups)],
        [smem, hbm],
        me,
        great,
        out_specs=[vmem()] * (groups * len(counts)),
        scratch=[
            pltpu.VMEM((e_dev, orbitals, orbitals), BF16),
            pltpu.VMEM((orbitals * e_dev, orbitals), F32),
            pltpu.SemaphoreType.DMA((4,)),
        ],
    )
    great = [exchange(parts[:groups])]
    rest = parts[groups:]
    less = call(
        spectrum_kernel,
        shape(fwd_e.shape[0], rows * orbitals, dtype=F32),
        [vmem()] * (1 + groups),
        fwd_e,
        *less,
        out_specs=vmem(),
        scratch=[pltpu.VMEM((total * rows, orbitals), F32)],
    )
    if len(counts) > 1:
        *rest, less = lax.optimization_barrier((*rest, less))
        great.append(exchange(rest))
    pol = [[] for _ in range(halves)]
    later = []
    for c, count in enumerate(counts):
        width = rows if c == len(counts) - 1 else count
        parts = call(
            functools.partial(pol_kernel, groups, halves, sum(counts[:c]), len(later)),
            [shape(lags, count, orbitals)] * groups
            + [shape(lags, width, orbitals)] * ((halves - 1) * groups),
            [vmem()] * (3 + groups + len(later)),
            fwd_e,
            back_l,
            less,
            *great[c],
            *later,
            out_specs=[vmem()] * (halves * groups),
            scratch=[pltpu.VMEM((total * count, orbitals), F32)],
        )
        pol[0].append(exchange(parts[:groups]))
        later += parts[groups:]
    for h in range(1, halves):
        last = len(later) - (halves - h) * groups
        pol[h].append(exchange(later[last : last + groups]))

    near_pairs = [(b, b ^ 1) for b in range(peers) if b ^ 1 < peers]
    far_pairs = [(b, ((b + 1) ^ 1) - 1) for b in range(1, peers) if ((b + 1) ^ 1) - 1 < peers]
    inter = []
    for h in range(halves):
        parts = [chunk[d] for d in range(groups) for chunk in pol[h]]
        own = call(
            assemble_kernel,
            shape(lags, orbitals, orbitals),
            [vmem()] * len(parts),
            *parts,
            out_specs=vmem(),
        )
        far = lax.ppermute(own, "block", far_pairs)
        near = lax.ppermute(own, "block", near_pairs)
        if h < halves - 1:
            partial = call(
                near_kernel,
                shape(lags, orbitals, orbitals, dtype=F32),
                [vmem()] * 4,
                near_left,
                near_right,
                own,
                near,
                out_specs=vmem(),
            )
            cut = [rows]
            parts = call(
                functools.partial(far_kernel, groups),
                [shape(count, lags, orbitals) for count in cut for _ in range(groups)],
                [smem] + [vmem()] * 4,
                me,
                far_left,
                far_right,
                partial,
                far,
                out_specs=[vmem()] * (groups * len(cut)),
                scratch=[pltpu.VMEM((orbitals * lags, orbitals), F32)],
            )
        else:
            cut = [rows]
            parts = call(
                functools.partial(all_kernel, groups),
                [shape(rows, lags, orbitals)] * groups,
                [smem] + [vmem()] * 7,
                me,
                near_left,
                near_right,
                far_left,
                far_right,
                own,
                near,
                far,
                out_specs=[vmem()] * groups,
                scratch=[pltpu.VMEM((orbitals * lags, orbitals), F32)],
            )
        inter.append(
            [exchange(parts[c * groups : (c + 1) * groups]) for c in range(len(cut))]
        )

    counts = [3 * rows // 4, rows // 4] if rows % 32 == 0 else [rows]
    sigma = []
    for c, count in enumerate(counts):
        first = sum(counts[:c])
        parts = call(
            functools.partial(sigma_kernel, groups, first, [first] * halves),
            [shape(count, e_dev, orbitals)] * groups,
            [vmem()] * (3 + groups * halves),
            fwd_l,
            back_e,
            less,
            *[part for half in inter for part in half[0]],
            out_specs=[vmem()] * groups,
        )
        sigma.append((first, count, exchange(parts)))
    out = []
    for first, count, parts in sigma:
        out = [
            call(
                functools.partial(final_kernel, groups, first),
                shape(e_dev, orbitals, orbitals, dtype=F32),
                [smem] + [vmem()] * groups + [hbm] * len(out),
                me,
                *parts,
                *out,
                out_specs=hbm,
                scratch=[
                    pltpu.VMEM((groups, e_dev * count, orbitals), F32),
                    pltpu.SemaphoreType.DMA((groups,)),
                ],
                input_output_aliases={1 + groups: 0} if out else {},
            )
        ]
    return out[0].reshape(e_dev, 1, orbitals, orbitals)


def solution(mesh):
    return jax.shard_map(
        shards,
        mesh=mesh,
        in_specs=(
            P("energy", "block", None, None),
            P("energy", "block", None, None),
            P("block", None, None, None),
            P("block", None),
        ),
        out_specs=P("energy", "block", None, None),
        check_vma=False,
    )
```

```python
import functools
import math

import jax
import jax.numpy as jnp
import numpy as np
from jax import lax
from jax.experimental import pallas as pl
from jax.experimental.pallas import tpu as pltpu
from jax.sharding import PartitionSpec as P

BF16 = jnp.bfloat16
F32 = jnp.float32


def split(table):
    upper = table.astype(BF16)
    lower = (table - upper.astype(np.float32)).astype(BF16)
    return upper, lower


def tables(groups, e_dev):
    total = groups * e_dev
    length = 3 * total // 2
    omega = 2.0 * math.pi / length * (np.arange(length // 2) + 0.5)
    scale = 2.0 / (length * math.sqrt(total))
    energies = np.arange(total)
    lags = energies - total // 2

    def forward(points):
        angle = omega[:, None] * points[None, :]
        table = np.concatenate([np.cos(angle), np.sin(angle)], axis=0).astype(np.float32)
        return np.concatenate(split(table), axis=1)

    def backward(points):
        angle = points[:, None] * omega[None, :]
        table = np.concatenate([np.cos(angle), np.sin(angle)], axis=1) * scale
        return np.concatenate(split(table.astype(np.float32)), axis=0)

    def ordered(me):
        return np.concatenate([np.arange(e_dev) + (me ^ d) * e_dev for d in range(groups)])

    fwd_e = np.stack([forward(energies[ordered(me)]) for me in range(groups)])
    fwd_l = np.stack([forward(lags[ordered(me)]) for me in range(groups)])
    back_l = np.stack([backward(lags[ordered(me)]) for me in range(groups)])
    back_e = np.stack([backward(energies[ordered(me)]) for me in range(groups)])
    return fwd_e, fwd_l, back_l, back_e


def params():
    return pltpu.CompilerParams(vmem_limit_bytes=12 * 1024 * 1024)


def vmem():
    return pl.BlockSpec(memory_space=pltpu.VMEM)


def dot(a, b):
    return jnp.dot(a, b, preferred_element_type=F32)


def slice_kernel(groups, me_ref, hbm, *rest):
    outs, sems = rest[:groups], rest[groups]
    rows = outs[0].shape[1]
    copies = []
    for d in range(groups):
        place = pl.ds(pl.multiple_of((me_ref[0] ^ d) * rows, rows), rows)
        copies.append(pltpu.make_async_copy(hbm.at[:, place], outs[d], sems.at[d]))
        copies[d].start()
    for copy in copies:
        copy.wait()


def turn_kernel(groups, counts, me_ref, hbm, *rest):
    outs = rest[: groups * len(counts)]
    x_ref, scratch, sems = rest[groups * len(counts) :]
    e_dev, orbitals, _ = x_ref.shape
    rows = orbitals // groups
    me = me_ref[0]
    span = e_dev // sems.shape[0]
    copies = []
    for p in range(sems.shape[0]):
        part = pl.ds(p * span, span)
        copies.append(pltpu.make_async_copy(hbm.at[part], x_ref.at[part], sems.at[p]))
        copies[p].start()
    for p, copy in enumerate(copies):
        copy.wait()
        for e in range(p * span, (p + 1) * span):
            scratch[pl.ds(e, orbitals, stride=e_dev), :] = x_ref[e].astype(F32).T
    first = 0
    for c, count in enumerate(counts):
        for d in range(groups):
            start = pl.multiple_of(((me ^ d) * rows + first) * e_dev, 8)
            part = scratch[pl.ds(start, count * e_dev), :]
            outs[c * groups + d][...] = part.astype(BF16).reshape(count, e_dev, orbitals)
        first += count


def gathered(refs, i, wide):
    both = jnp.concatenate(
        [jnp.concatenate([ref[i + h] for ref in refs], axis=0) for h in range(wide)], axis=1
    )
    return jnp.concatenate([both, both], axis=0)


def inverse(back, spectrum):
    both = dot(back, spectrum.astype(BF16))
    half = both.shape[0] // 2
    return both[:half] + both[half:]


def spectrum_kernel(fwd_ref, *refs):
    less, out, scratch = refs[:-2], refs[-2], refs[-1]
    e_dev, rows, orbitals = less[0].shape
    size = e_dev * rows
    for d, part in enumerate(less):
        scratch[d * size : (d + 1) * size, :] = part[...].astype(F32).reshape(size, orbitals)
    total = e_dev * len(less)
    both = jnp.concatenate(
        [scratch[pl.ds(i, total, stride=rows), :] for i in range(rows)], axis=1
    ).astype(BF16)
    out[...] = dot(fwd_ref[...], jnp.concatenate([both, both], axis=0))


def pol_kernel(groups, halves, first, earlier, fwd_ref, back_ref, less_ref, *refs):
    great, before = refs[:groups], refs[groups : groups + earlier]
    outs, scratch = refs[groups + earlier : -1], refs[-1]
    count, e_dev, orbitals = great[0].shape
    freq = fwd_ref.shape[0] // 2
    fwd, back = fwd_ref[...], back_ref[...]
    total = groups * e_dev
    wide = count
    for i in range(0, count, wide):
        a = less_ref[:, (first + i) * orbitals : (first + i + wide) * orbitals]
        b = dot(fwd, gathered(great, i, wide))
        real = a[:freq] * b[:freq] + a[freq:] * b[freq:]
        imag = a[freq:] * b[:freq] - a[:freq] * b[freq:]
        pol = inverse(back, jnp.concatenate([real, imag], axis=0))
        for h in range(wide):
            scratch[pl.ds(i + h, total, stride=count), :] = pol[
                :, h * orbitals : (h + 1) * orbitals
            ]
    lags = e_dev // halves

    def part(d, h):
        start = (d * halves + h) * lags * count
        return scratch[start : start + lags * count, :].astype(BF16).reshape(lags, count, orbitals)

    for d in range(groups):
        outs[d][...] = part(d, 0)
        for h in range(1, halves):
            out = outs[h * groups + d]
            at = 0
            for ref in before[(h - 1) * groups + d :: (halves - 1) * groups]:
                out[:, at : at + ref.shape[1], :] = ref[...]
                at += ref.shape[1]
            out[:, at:, :] = part(d, h)


def sigma_kernel(groups, first, offsets, fwd_l_ref, back_ref, less_ref, *refs):
    halves = len(offsets)
    inter, outs = refs[: groups * halves], refs[groups * halves :]
    count, e_dev, orbitals = outs[0].shape
    freq = fwd_l_ref.shape[0] // 2
    fwd_l, back = fwd_l_ref[...], back_ref[...]
    inter = [
        inter[h * groups + d].at[offsets[h] : offsets[h] + count]
        for d in range(groups)
        for h in range(halves)
    ]
    wide = count
    for i in range(0, count, wide):
        a = less_ref[:, (first + i) * orbitals : (first + i + wide) * orbitals]
        b = dot(fwd_l, gathered(inter, i, wide))
        real = a[:freq] * b[:freq] - a[freq:] * b[freq:]
        imag = a[freq:] * b[:freq] + a[:freq] * b[freq:]
        sigma = inverse(back, jnp.concatenate([real, imag], axis=0)).astype(BF16)
        for h in range(wide):
            for d in range(groups):
                outs[d][i + h] = sigma[
                    d * e_dev : (d + 1) * e_dev, h * orbitals : (h + 1) * orbitals
                ]


def assemble_kernel(*refs):
    ins, out = refs[:-1], refs[-1]
    at = 0
    for part in ins:
        out[:, at : at + part.shape[1], :] = part[...]
        at += part.shape[1]


def diagonal(a, b):
    zero = jnp.zeros_like(a)
    return jnp.concatenate(
        [jnp.concatenate([a, zero], axis=1), jnp.concatenate([zero, b], axis=1)], axis=0
    )


def setup_kernel(groups, count, me_ref, odd_ref, mask_ref, v_ref, *refs):
    sources, outs = refs[:count], refs[count : 2 * count]
    left, pair_right, far_right, scratch, sems = refs[2 * count :]
    me = me_ref[0]
    copies = [
        pltpu.make_async_copy(src.at[me], dst, sems.at[n])
        for n, (src, dst) in enumerate(zip(sources, outs))
    ]
    for copy in copies:
        copy.start()
    odd = odd_ref[0]
    scratch[0] = v_ref[1].astype(F32).T
    scratch[1] = v_ref[2 - 2 * odd].astype(F32).T
    scratch[2] = v_ref[2 * odd].astype(F32).T
    rows = scratch.shape[1] // groups

    def ordered(n):
        parts = [
            scratch[n, pl.ds(pl.multiple_of((me ^ d) * rows, rows), rows), :] for d in range(groups)
        ]
        return jnp.concatenate(parts, axis=0).T.astype(BF16)

    def masked(n, t):
        return (scratch[n] * mask_ref[t].astype(F32)).astype(BF16)

    left[...] = jnp.concatenate([ordered(0), ordered(1), ordered(2)], axis=1)
    pair_right[...] = diagonal(scratch[0].astype(BF16), masked(1, 1 - odd))
    far_right[...] = masked(2, odd)
    for copy in copies:
        copy.wait()


def screen_kernel(groups, me_ref, left, pair_right, far_right, own, near, far, *refs):
    outs, scratch = refs[:-1], refs[-1]
    lags, n, _ = far.shape
    rows = n // groups
    me = me_ref[0]
    both = jnp.concatenate([own[...].reshape(lags * n, n), near[...].reshape(lags * n, n)], axis=1)
    half = dot(both, pair_right[...]).astype(BF16)
    other = dot(far[...].reshape(lags * n, n), far_right[...]).astype(BF16)
    half = jnp.concatenate(
        [
            jnp.concatenate(
                [
                    half[k * n : k * n + n, :n],
                    half[k * n : k * n + n, n:],
                    other[k * n : k * n + n],
                ],
                axis=0,
            )
            for k in range(lags)
        ],
        axis=1,
    )
    terms = dot(left[...], half)
    for k in range(lags):
        scratch[pl.ds(k, n, stride=lags), :] = terms[:, k * n : k * n + n]
    first = 0
    for c in range(0, len(outs), groups):
        count = outs[c].shape[0]
        for d in range(groups):
            start = pl.multiple_of(((me ^ d) * rows + first) * lags, 8)
            part = scratch[pl.ds(start, count * lags), :]
            outs[c + d][...] = part.astype(BF16).reshape(count, lags, n)
        first += count


def final_kernel(groups, first, me_ref, *refs):
    ins, out, scratch, sems = refs[:groups], refs[-3], refs[-2], refs[-1]
    count, e_dev, orbitals = ins[0].shape
    rows = orbitals // groups
    me = me_ref[0]
    copies = []
    for d in range(groups):
        for i in range(count):
            scratch[d, pl.ds(i, e_dev, stride=count), :] = ins[d][i].astype(F32)
        start = pl.multiple_of((me ^ d) * rows + first, 8)
        copies.append(
            pltpu.make_async_copy(
                scratch.at[d].reshape(e_dev, count, orbitals),
                out.at[:, pl.ds(start, count), :],
                sems.at[d],
            )
        )
        copies[-1].start()
    for copy in copies:
        copy.wait()


def exchange(parts):
    groups = lax.axis_size("energy")
    moved = [parts[0]]
    for d in range(1, groups):
        moved.append(lax.ppermute(parts[d], "energy", [(i, i ^ d) for i in range(groups)]))
    return moved


def call(kernel, out_shape, specs, *args, scratch=(), **kwargs):
    return pl.pallas_call(
        kernel,
        out_shape=out_shape,
        in_specs=specs,
        scratch_shapes=list(scratch),
        compiler_params=params(),
        **kwargs,
    )(*args)


def shards(g_less, g_great, coupling, coupling_mask):
    e_dev, _, orbitals, _ = g_less.shape
    groups = lax.axis_size("energy")
    peers = lax.axis_size("block")
    rows = orbitals // groups
    total = e_dev * groups
    halves = 2 if e_dev % 32 == 0 else 1
    lags = e_dev // halves
    index = lax.axis_index("energy")
    me = index.astype(jnp.int32)[None]
    odd = (lax.axis_index("block") % 2).astype(jnp.int32)[None]
    smem = pl.BlockSpec(memory_space=pltpu.SMEM)
    hbm = pl.BlockSpec(memory_space=pltpu.HBM)

    def shape(*dims, dtype=BF16):
        return jax.ShapeDtypeStruct(dims, dtype)

    less = g_less.reshape(e_dev, orbitals, orbitals)
    great = g_great.reshape(e_dev, orbitals, orbitals)
    less, great = [pltpu.with_memory_space_constraint(x, pltpu.HBM) for x in (less, great)]

    parts = [shape(e_dev, rows, orbitals)] * groups
    less = call(
        functools.partial(slice_kernel, groups),
        parts,
        [smem, hbm],
        me,
        less,
        out_specs=[vmem()] * groups,
        scratch=[pltpu.SemaphoreType.DMA((groups,))],
    )
    less = exchange(less)
    stacks = [pltpu.with_memory_space_constraint(jnp.asarray(t), pltpu.HBM) for t in tables(groups, e_dev)]
    square = (orbitals, orbitals)
    fwd_e, fwd_l, back_l, back_e, left, pair_right, far_right = call(
        functools.partial(setup_kernel, groups, len(stacks)),
        [shape(*t.shape[1:]) for t in stacks]
        + [shape(orbitals, 3 * orbitals), shape(2 * orbitals, 2 * orbitals), shape(*square)],
        [smem, smem, smem, vmem()] + [hbm] * len(stacks),
        me,
        odd,
        coupling_mask[0],
        coupling[0],
        *stacks,
        out_specs=[vmem()] * (len(stacks) + 3),
        scratch=[pltpu.VMEM((3, *square), F32), pltpu.SemaphoreType.DMA((len(stacks),))],
    )
    counts = [rows // 2, rows // 2] if rows % 32 == 0 else [rows]
    parts = call(
        functools.partial(turn_kernel, groups, counts),
        [shape(count, e_dev, orbitals) for count in counts for _ in range(groups)],
        [smem, hbm],
        me,
        great,
        out_specs=[vmem()] * (groups * len(counts)),
        scratch=[
            pltpu.VMEM((e_dev, orbitals, orbitals), BF16),
            pltpu.VMEM((orbitals * e_dev, orbitals), F32),
            pltpu.SemaphoreType.DMA((4,)),
        ],
    )
    great = [exchange(parts[:groups])]
    rest = parts[groups:]
    less = call(
        spectrum_kernel,
        shape(fwd_e.shape[0], rows * orbitals, dtype=F32),
        [vmem()] * (1 + groups),
        fwd_e,
        *less,
        out_specs=vmem(),
        scratch=[pltpu.VMEM((total * rows, orbitals), F32)],
    )
    if len(counts) > 1:
        *rest, less = lax.optimization_barrier((*rest, less))
        great.append(exchange(rest))
    pol = [[] for _ in range(halves)]
    later = []
    for c, count in enumerate(counts):
        width = rows if c == len(counts) - 1 else count
        parts = call(
            functools.partial(pol_kernel, groups, halves, sum(counts[:c]), len(later)),
            [shape(lags, count, orbitals)] * groups
            + [shape(lags, width, orbitals)] * ((halves - 1) * groups),
            [vmem()] * (3 + groups + len(later)),
            fwd_e,
            back_l,
            less,
            *great[c],
            *later,
            out_specs=[vmem()] * (halves * groups),
            scratch=[pltpu.VMEM((total * count, orbitals), F32)],
        )
        pol[0].append(exchange(parts[:groups]))
        later += parts[groups:]
    for h in range(1, halves):
        last = len(later) - (halves - h) * groups
        pol[h].append(exchange(later[last : last + groups]))

    near_pairs = [(b, b ^ 1) for b in range(peers) if b ^ 1 < peers]
    far_pairs = [(b, ((b + 1) ^ 1) - 1) for b in range(1, peers) if ((b + 1) ^ 1) - 1 < peers]
    inter = []
    for h in range(halves):
        parts = [chunk[d] for d in range(groups) for chunk in pol[h]]
        own = call(
            assemble_kernel,
            shape(lags, orbitals, orbitals),
            [vmem()] * len(parts),
            *parts,
            out_specs=vmem(),
        )
        far = lax.ppermute(own, "block", far_pairs)
        near = lax.ppermute(own, "block", near_pairs)
        parts = call(
            functools.partial(screen_kernel, groups),
            [shape(rows, lags, orbitals)] * groups,
            [smem] + [vmem()] * 6,
            me,
            left,
            pair_right,
            far_right,
            own,
            near,
            far,
            out_specs=[vmem()] * groups,
            scratch=[pltpu.VMEM((orbitals * lags, orbitals), F32)],
        )
        inter.append(exchange(parts))

    counts = [3 * rows // 4, rows // 4] if rows % 32 == 0 else [rows]
    sigma = []
    for c, count in enumerate(counts):
        first = sum(counts[:c])
        parts = call(
            functools.partial(sigma_kernel, groups, first, [first] * halves),
            [shape(count, e_dev, orbitals)] * groups,
            [vmem()] * (3 + groups * halves),
            fwd_l,
            back_e,
            less,
            *[part for half in inter for part in half],
            out_specs=[vmem()] * groups,
        )
        sigma.append((first, count, exchange(parts)))
    out = []
    for first, count, parts in sigma:
        out = [
            call(
                functools.partial(final_kernel, groups, first),
                shape(e_dev, orbitals, orbitals, dtype=F32),
                [smem] + [vmem()] * groups + [hbm] * len(out),
                me,
                *parts,
                *out,
                out_specs=hbm,
                scratch=[
                    pltpu.VMEM((groups, e_dev * count, orbitals), F32),
                    pltpu.SemaphoreType.DMA((groups,)),
                ],
                input_output_aliases={1 + groups: 0} if out else {},
            )
        ]
    return out[0].reshape(e_dev, 1, orbitals, orbitals)


def solution(mesh):
    return jax.shard_map(
        shards,
        mesh=mesh,
        in_specs=(
            P("energy", "block", None, None),
            P("energy", "block", None, None),
            P("block", None, None, None),
            P("block", None),
        ),
        out_specs=P("energy", "block", None, None),
        check_vma=False,
    )
```

```python
import functools
import math

import jax
import jax.numpy as jnp
import numpy as np
from jax import lax
from jax.experimental import pallas as pl
from jax.experimental.pallas import tpu as pltpu
from jax.sharding import PartitionSpec as P

BF16 = jnp.bfloat16
F32 = jnp.float32


def split(table):
    upper = table.astype(BF16)
    lower = (table - upper.astype(np.float32)).astype(BF16)
    return upper, lower


def tables(groups, e_dev):
    total = groups * e_dev
    length = 3 * total // 2
    omega = 2.0 * math.pi / length * (np.arange(length // 2) + 0.5)
    scale = 2.0 / (length * math.sqrt(total))
    energies = np.arange(total)
    lags = energies - total // 2

    def forward(points):
        angle = omega[:, None] * points[None, :]
        table = np.concatenate([np.cos(angle), np.sin(angle)], axis=0).astype(np.float32)
        return np.concatenate(split(table), axis=1)

    def backward(points):
        angle = points[:, None] * omega[None, :]
        table = np.concatenate([np.cos(angle), np.sin(angle)], axis=1) * scale
        return np.concatenate(split(table.astype(np.float32)), axis=0)

    def ordered(me):
        return np.concatenate([np.arange(e_dev) + (me ^ d) * e_dev for d in range(groups)])

    fwd_e = np.stack([forward(energies[ordered(me)]) for me in range(groups)])
    fwd_l = np.stack([forward(lags[ordered(me)]) for me in range(groups)])
    back_l = np.stack([backward(lags[ordered(me)]) for me in range(groups)])
    back_e = np.stack([backward(energies[ordered(me)]) for me in range(groups)])
    return fwd_e, fwd_l, back_l, back_e


def params():
    return pltpu.CompilerParams(vmem_limit_bytes=12 * 1024 * 1024)


def vmem():
    return pl.BlockSpec(memory_space=pltpu.VMEM)


def dot(a, b):
    return jnp.dot(a, b, preferred_element_type=F32)


def slice_kernel(groups, me_ref, hbm, *rest):
    outs, sems = rest[:groups], rest[groups]
    rows = outs[0].shape[1]
    copies = []
    for d in range(groups):
        place = pl.ds(pl.multiple_of((me_ref[0] ^ d) * rows, rows), rows)
        copies.append(pltpu.make_async_copy(hbm.at[:, place], outs[d], sems.at[d]))
        copies[d].start()
    for copy in copies:
        copy.wait()


def turn_kernel(groups, counts, me_ref, hbm, *rest):
    outs = rest[: groups * len(counts)]
    x_ref, scratch, sems = rest[groups * len(counts) :]
    e_dev, orbitals, _ = x_ref.shape
    rows = orbitals // groups
    me = me_ref[0]
    span = e_dev // sems.shape[0]
    copies = []
    for p in range(sems.shape[0]):
        part = pl.ds(p * span, span)
        copies.append(pltpu.make_async_copy(hbm.at[part], x_ref.at[part], sems.at[p]))
        copies[p].start()
    for p, copy in enumerate(copies):
        copy.wait()
        for e in range(p * span, (p + 1) * span):
            scratch[pl.ds(e, orbitals, stride=e_dev), :] = x_ref[e].astype(F32).T
    first = 0
    for c, count in enumerate(counts):
        for d in range(groups):
            start = pl.multiple_of(((me ^ d) * rows + first) * e_dev, 8)
            part = scratch[pl.ds(start, count * e_dev), :]
            outs[c * groups + d][...] = part.astype(BF16).reshape(count, e_dev, orbitals)
        first += count


def gathered(refs, i, wide):
    both = jnp.concatenate(
        [jnp.concatenate([ref[i + h] for ref in refs], axis=0) for h in range(wide)], axis=1
    )
    return jnp.concatenate([both, both], axis=0)


def inverse(back, spectrum):
    both = dot(back, spectrum.astype(BF16))
    half = both.shape[0] // 2
    return both[:half] + both[half:]


def spectrum_kernel(fwd_ref, *refs):
    less, out, scratch = refs[:-2], refs[-2], refs[-1]
    e_dev, rows, orbitals = less[0].shape
    size = e_dev * rows
    for d, part in enumerate(less):
        scratch[d * size : (d + 1) * size, :] = part[...].astype(F32).reshape(size, orbitals)
    total = e_dev * len(less)
    both = jnp.concatenate(
        [scratch[pl.ds(i, total, stride=rows), :] for i in range(rows)], axis=1
    ).astype(BF16)
    out[...] = dot(fwd_ref[...], jnp.concatenate([both, both], axis=0))


def pol_kernel(groups, halves, first, earlier, fwd_ref, back_ref, less_ref, *refs):
    great, before = refs[:groups], refs[groups : groups + earlier]
    outs, scratch = refs[groups + earlier : -1], refs[-1]
    count, e_dev, orbitals = great[0].shape
    freq = fwd_ref.shape[0] // 2
    fwd, back = fwd_ref[...], back_ref[...]
    total = groups * e_dev
    wide = count
    for i in range(0, count, wide):
        a = less_ref[:, (first + i) * orbitals : (first + i + wide) * orbitals]
        b = dot(fwd, gathered(great, i, wide))
        real = a[:freq] * b[:freq] + a[freq:] * b[freq:]
        imag = a[freq:] * b[:freq] - a[:freq] * b[freq:]
        pol = inverse(back, jnp.concatenate([real, imag], axis=0))
        for h in range(wide):
            scratch[pl.ds(i + h, total, stride=count), :] = pol[
                :, h * orbitals : (h + 1) * orbitals
            ]
    lags = e_dev // halves

    def part(d, h):
        start = (d * halves + h) * lags * count
        return scratch[start : start + lags * count, :].astype(BF16).reshape(lags, count, orbitals)

    for d in range(groups):
        outs[d][...] = part(d, 0)
        for h in range(1, halves):
            out = outs[h * groups + d]
            at = 0
            for ref in before[(h - 1) * groups + d :: (halves - 1) * groups]:
                out[:, at : at + ref.shape[1], :] = ref[...]
                at += ref.shape[1]
            out[:, at:, :] = part(d, h)


def sigma_kernel(groups, first, offsets, fwd_l_ref, back_ref, less_ref, *refs):
    halves = len(offsets)
    inter, outs = refs[: groups * halves], refs[groups * halves :]
    count, e_dev, orbitals = outs[0].shape
    freq = fwd_l_ref.shape[0] // 2
    fwd_l, back = fwd_l_ref[...], back_ref[...]
    inter = [
        inter[h * groups + d].at[offsets[h] : offsets[h] + count]
        for d in range(groups)
        for h in range(halves)
    ]
    wide = count
    for i in range(0, count, wide):
        a = less_ref[:, (first + i) * orbitals : (first + i + wide) * orbitals]
        b = dot(fwd_l, gathered(inter, i, wide))
        real = a[:freq] * b[:freq] - a[freq:] * b[freq:]
        imag = a[freq:] * b[:freq] + a[:freq] * b[freq:]
        sigma = inverse(back, jnp.concatenate([real, imag], axis=0)).astype(BF16)
        for h in range(wide):
            for d in range(groups):
                outs[d][i + h] = sigma[
                    d * e_dev : (d + 1) * e_dev, h * orbitals : (h + 1) * orbitals
                ]


def assemble_kernel(groups, *refs):
    out = refs[-1]
    ins = [part for d in range(groups) for part in refs[d:-1:groups]]
    at = 0
    for part in ins:
        out[:, at : at + part.shape[1], :] = part[...]
        at += part.shape[1]


def diagonal(a, b):
    zero = jnp.zeros_like(a)
    return jnp.concatenate(
        [jnp.concatenate([a, zero], axis=1), jnp.concatenate([zero, b], axis=1)], axis=0
    )


def setup_kernel(groups, count, me_ref, odd_ref, mask_ref, v_ref, *refs):
    sources, outs = refs[:count], refs[count : 2 * count]
    left, pair_right, far_right, scratch, sems = refs[2 * count :]
    me = me_ref[0]
    copies = [
        pltpu.make_async_copy(src.at[me], dst, sems.at[n])
        for n, (src, dst) in enumerate(zip(sources, outs))
    ]
    for copy in copies:
        copy.start()
    odd = odd_ref[0]
    scratch[0] = v_ref[1].astype(F32).T
    scratch[1] = v_ref[2 - 2 * odd].astype(F32).T
    scratch[2] = v_ref[2 * odd].astype(F32).T
    rows = scratch.shape[1] // groups

    def ordered(n):
        parts = [
            scratch[n, pl.ds(pl.multiple_of((me ^ d) * rows, rows), rows), :] for d in range(groups)
        ]
        return jnp.concatenate(parts, axis=0).T.astype(BF16)

    def masked(n, t):
        return (scratch[n] * mask_ref[t].astype(F32)).astype(BF16)

    left[...] = jnp.concatenate([ordered(0), ordered(1), ordered(2)], axis=1)
    pair_right[...] = diagonal(scratch[0].astype(BF16), masked(1, 1 - odd))
    far_right[...] = masked(2, odd)
    for copy in copies:
        copy.wait()


def screen_kernel(groups, me_ref, left, pair_right, far_right, own, near, far, *refs):
    outs, scratch = refs[:-1], refs[-1]
    lags, n, _ = far.shape
    rows = n // groups
    me = me_ref[0]
    both = jnp.concatenate([own[...].reshape(lags * n, n), near[...].reshape(lags * n, n)], axis=1)
    half = dot(both, pair_right[...]).astype(BF16)
    other = dot(far[...].reshape(lags * n, n), far_right[...]).astype(BF16)
    half = jnp.concatenate(
        [
            jnp.concatenate(
                [
                    half[k * n : k * n + n, :n],
                    half[k * n : k * n + n, n:],
                    other[k * n : k * n + n],
                ],
                axis=0,
            )
            for k in range(lags)
        ],
        axis=1,
    )
    terms = dot(left[...], half)
    for k in range(lags):
        scratch[pl.ds(k, n, stride=lags), :] = terms[:, k * n : k * n + n]
    first = 0
    for c in range(0, len(outs), groups):
        count = outs[c].shape[0]
        for d in range(groups):
            start = pl.multiple_of(((me ^ d) * rows + first) * lags, 8)
            part = scratch[pl.ds(start, count * lags), :]
            outs[c + d][...] = part.astype(BF16).reshape(count, lags, n)
        first += count


def final_kernel(groups, pieces, me_ref, *refs):
    ins, out = refs[: len(pieces)], refs[-len(pieces) - 2]
    scratch, sems = refs[-len(pieces) - 1 : -1], refs[-1]
    me = me_ref[0]
    copies = []
    for n, (d, first) in enumerate(pieces):
        count, e_dev, orbitals = ins[n].shape
        rows = orbitals // groups
        for i in range(count):
            scratch[n][pl.ds(i, e_dev, stride=count), :] = ins[n][i].astype(F32)
        start = pl.multiple_of((me ^ d) * rows + first, 8)
        copies.append(
            pltpu.make_async_copy(
                scratch[n].reshape(e_dev, count, orbitals),
                out.at[:, pl.ds(start, count), :],
                sems.at[n],
            )
        )
        copies[-1].start()
    for copy in copies:
        copy.wait()


def exchange(parts):
    groups = lax.axis_size("energy")
    moved = [parts[0]]
    for d in range(1, groups):
        moved.append(lax.ppermute(parts[d], "energy", [(i, i ^ d) for i in range(groups)]))
    return moved


def call(kernel, out_shape, specs, *args, scratch=(), **kwargs):
    return pl.pallas_call(
        kernel,
        out_shape=out_shape,
        in_specs=specs,
        scratch_shapes=list(scratch),
        compiler_params=params(),
        **kwargs,
    )(*args)


def shards(g_less, g_great, coupling, coupling_mask):
    e_dev, _, orbitals, _ = g_less.shape
    groups = lax.axis_size("energy")
    peers = lax.axis_size("block")
    rows = orbitals // groups
    total = e_dev * groups
    halves = 2 if e_dev % 32 == 0 else 1
    lags = e_dev // halves
    index = lax.axis_index("energy")
    me = index.astype(jnp.int32)[None]
    odd = (lax.axis_index("block") % 2).astype(jnp.int32)[None]
    smem = pl.BlockSpec(memory_space=pltpu.SMEM)
    hbm = pl.BlockSpec(memory_space=pltpu.HBM)

    def shape(*dims, dtype=BF16):
        return jax.ShapeDtypeStruct(dims, dtype)

    less = g_less.reshape(e_dev, orbitals, orbitals)
    great = g_great.reshape(e_dev, orbitals, orbitals)
    less, great = [pltpu.with_memory_space_constraint(x, pltpu.HBM) for x in (less, great)]

    parts = [shape(e_dev, rows, orbitals)] * groups
    less = call(
        functools.partial(slice_kernel, groups),
        parts,
        [smem, hbm],
        me,
        less,
        out_specs=[vmem()] * groups,
        scratch=[pltpu.SemaphoreType.DMA((groups,))],
    )
    less = exchange(less)
    stacks = [pltpu.with_memory_space_constraint(jnp.asarray(t), pltpu.HBM) for t in tables(groups, e_dev)]
    square = (orbitals, orbitals)
    fwd_e, fwd_l, back_l, back_e, left, pair_right, far_right = call(
        functools.partial(setup_kernel, groups, len(stacks)),
        [shape(*t.shape[1:]) for t in stacks]
        + [shape(orbitals, 3 * orbitals), shape(2 * orbitals, 2 * orbitals), shape(*square)],
        [smem, smem, smem, vmem()] + [hbm] * len(stacks),
        me,
        odd,
        coupling_mask[0],
        coupling[0],
        *stacks,
        out_specs=[vmem()] * (len(stacks) + 3),
        scratch=[pltpu.VMEM((3, *square), F32), pltpu.SemaphoreType.DMA((len(stacks),))],
    )
    counts = [rows // 2, rows // 2] if rows % 32 == 0 else [rows]
    parts = call(
        functools.partial(turn_kernel, groups, counts),
        [shape(count, e_dev, orbitals) for count in counts for _ in range(groups)],
        [smem, hbm],
        me,
        great,
        out_specs=[vmem()] * (groups * len(counts)),
        scratch=[
            pltpu.VMEM((e_dev, orbitals, orbitals), BF16),
            pltpu.VMEM((orbitals * e_dev, orbitals), F32),
            pltpu.SemaphoreType.DMA((4,)),
        ],
    )
    great = [exchange(parts[:groups])]
    rest = parts[groups:]
    less = call(
        spectrum_kernel,
        shape(fwd_e.shape[0], rows * orbitals, dtype=F32),
        [vmem()] * (1 + groups),
        fwd_e,
        *less,
        out_specs=vmem(),
        scratch=[pltpu.VMEM((total * rows, orbitals), F32)],
    )
    if len(counts) > 1:
        *rest, less = lax.optimization_barrier((*rest, less))
        great.append(exchange(rest))
    pol = [[] for _ in range(halves)]
    later = []
    for c, count in enumerate(counts):
        width = rows if c == len(counts) - 1 else count
        parts = call(
            functools.partial(pol_kernel, groups, halves, sum(counts[:c]), len(later)),
            [shape(lags, count, orbitals)] * groups
            + [shape(lags, width, orbitals)] * ((halves - 1) * groups),
            [vmem()] * (3 + groups + len(later)),
            fwd_e,
            back_l,
            less,
            *great[c],
            *later,
            out_specs=[vmem()] * (halves * groups),
            scratch=[pltpu.VMEM((total * count, orbitals), F32)],
        )
        pol[0].append(exchange(parts[:groups]))
        later += parts[groups:]
    for h in range(1, halves):
        last = len(later) - (halves - h) * groups
        pol[h].append(exchange(later[last : last + groups]))

    near_pairs = [(b, b ^ 1) for b in range(peers) if b ^ 1 < peers]
    far_pairs = [(b, ((b + 1) ^ 1) - 1) for b in range(1, peers) if ((b + 1) ^ 1) - 1 < peers]
    inter = []
    for h in range(halves):
        parts = [part for chunk in pol[h] for part in chunk]
        own = call(
            functools.partial(assemble_kernel, groups),
            shape(lags, orbitals, orbitals),
            [vmem()] * len(parts),
            *parts,
            out_specs=vmem(),
        )
        far = lax.ppermute(own, "block", far_pairs)
        near = lax.ppermute(own, "block", near_pairs)
        parts = call(
            functools.partial(screen_kernel, groups),
            [shape(rows, lags, orbitals)] * groups,
            [smem] + [vmem()] * 6,
            me,
            left,
            pair_right,
            far_right,
            own,
            near,
            far,
            out_specs=[vmem()] * groups,
            scratch=[pltpu.VMEM((orbitals * lags, orbitals), F32)],
        )
        inter.append(exchange(parts))

    counts = [3 * rows // 4, rows // 4] if rows % 32 == 0 else [rows]
    sigma = []
    for c, count in enumerate(counts):
        first = sum(counts[:c])
        parts = call(
            functools.partial(sigma_kernel, groups, first, [first] * halves),
            [shape(count, e_dev, orbitals)] * groups,
            [vmem()] * (3 + groups * halves),
            fwd_l,
            back_e,
            less,
            *[part for half in inter for part in half],
            out_specs=[vmem()] * groups,
        )
        sigma.append((first, count, exchange(parts)))
    pieces = [[(d, first, part) for d, part in enumerate(parts)] for first, _, parts in sigma]
    if len(pieces) > 1:
        pieces[-2].append(pieces[-1].pop(0))
    out = []
    for group in pieces:
        out = [
            call(
                functools.partial(final_kernel, groups, [(d, first) for d, first, _ in group]),
                shape(e_dev, orbitals, orbitals, dtype=F32),
                [smem] + [vmem()] * len(group) + [hbm] * len(out),
                me,
                *[part for _, _, part in group],
                *out,
                out_specs=hbm,
                scratch=[
                    pltpu.VMEM((e_dev * part.shape[0], orbitals), F32) for _, _, part in group
                ]
                + [pltpu.SemaphoreType.DMA((len(group),))],
                input_output_aliases={1 + len(group): 0} if out else {},
            )
        ]
    return out[0].reshape(e_dev, 1, orbitals, orbitals)


def solution(mesh):
    return jax.shard_map(
        shards,
        mesh=mesh,
        in_specs=(
            P("energy", "block", None, None),
            P("energy", "block", None, None),
            P("block", None, None, None),
            P("block", None),
        ),
        out_specs=P("energy", "block", None, None),
        check_vma=False,
    )
```

```python
import functools
import math

import jax
import jax.numpy as jnp
import numpy as np
from jax import lax
from jax.experimental import pallas as pl
from jax.experimental.pallas import tpu as pltpu
from jax.sharding import PartitionSpec as P

BF16 = jnp.bfloat16
F32 = jnp.float32


def split(table):
    upper = table.astype(BF16)
    lower = (table - upper.astype(np.float32)).astype(BF16)
    return upper, lower


def tables(groups, e_dev):
    total = groups * e_dev
    length = 3 * total // 2
    omega = 2.0 * math.pi / length * (np.arange(length // 2) + 0.5)
    scale = 2.0 / (length * math.sqrt(total))
    energies = np.arange(total)
    lags = energies - total // 2

    def forward(points):
        angle = omega[:, None] * points[None, :]
        table = np.concatenate([np.cos(angle), np.sin(angle)], axis=0).astype(np.float32)
        return np.concatenate(split(table), axis=1)

    def backward(points):
        angle = points[:, None] * omega[None, :]
        table = np.concatenate([np.cos(angle), np.sin(angle)], axis=1) * scale
        return np.concatenate(split(table.astype(np.float32)), axis=0)

    def ordered(me):
        return np.concatenate([np.arange(e_dev) + (me ^ d) * e_dev for d in range(groups)])

    fwd_e = np.stack([forward(energies[ordered(me)]) for me in range(groups)])
    fwd_l = np.stack([forward(lags[ordered(me)]) for me in range(groups)])
    back_l = np.stack([backward(lags[ordered(me)]) for me in range(groups)])
    back_e = np.stack([backward(energies[ordered(me)]) for me in range(groups)])
    return fwd_e, fwd_l, back_l, back_e


def params():
    return pltpu.CompilerParams(vmem_limit_bytes=16 * 1024 * 1024)


def vmem():
    return pl.BlockSpec(memory_space=pltpu.VMEM)


def dot(a, b):
    return jnp.dot(a, b, preferred_element_type=F32)


def slice_kernel(groups, me_ref, hbm, *rest):
    outs, sems = rest[:groups], rest[groups]
    rows = outs[0].shape[1]
    copies = []
    for d in range(groups):
        place = pl.ds(pl.multiple_of((me_ref[0] ^ d) * rows, rows), rows)
        copies.append(pltpu.make_async_copy(hbm.at[:, place], outs[d], sems.at[d]))
        copies[d].start()
    for copy in copies:
        copy.wait()


def turn_kernel(groups, counts, me_ref, hbm, *rest):
    outs = rest[: groups * len(counts)]
    x_ref, scratch, sems = rest[groups * len(counts) :]
    e_dev, orbitals, _ = x_ref.shape
    rows = orbitals // groups
    me = me_ref[0]
    span = e_dev // sems.shape[0]
    copies = []
    for p in range(sems.shape[0]):
        part = pl.ds(p * span, span)
        copies.append(pltpu.make_async_copy(hbm.at[part], x_ref.at[part], sems.at[p]))
        copies[p].start()
    for p, copy in enumerate(copies):
        copy.wait()
        for e in range(p * span, (p + 1) * span):
            scratch[pl.ds(e, orbitals, stride=e_dev), :] = x_ref[e].astype(F32).T
    first = 0
    for c, count in enumerate(counts):
        for d in range(groups):
            start = pl.multiple_of(((me ^ d) * rows + first) * e_dev, 8)
            part = scratch[pl.ds(start, count * e_dev), :]
            outs[c * groups + d][...] = part.astype(BF16).reshape(count, e_dev, orbitals)
        first += count


def gathered(refs, i, wide):
    both = jnp.concatenate(
        [jnp.concatenate([ref[i + h] for ref in refs], axis=0) for h in range(wide)], axis=1
    )
    return jnp.concatenate([both, both], axis=0)


def inverse(back, spectrum):
    both = dot(back, spectrum.astype(BF16))
    half = both.shape[0] // 2
    return both[:half] + both[half:]


def spectrum_kernel(fwd_ref, *refs):
    less, out, scratch = refs[:-2], refs[-2], refs[-1]
    e_dev, rows, orbitals = less[0].shape
    size = e_dev * rows
    for d, part in enumerate(less):
        scratch[d * size : (d + 1) * size, :] = part[...].astype(F32).reshape(size, orbitals)
    total = e_dev * len(less)
    both = jnp.concatenate(
        [scratch[pl.ds(i, total, stride=rows), :] for i in range(rows)], axis=1
    ).astype(BF16)
    out[...] = dot(fwd_ref[...], jnp.concatenate([both, both], axis=0))


def pol_kernel(groups, halves, first, earlier, fwd_ref, back_ref, less_ref, *refs):
    great, before = refs[:groups], refs[groups : groups + earlier]
    outs, scratch = refs[groups + earlier : -1], refs[-1]
    count, e_dev, orbitals = great[0].shape
    freq = fwd_ref.shape[0] // 2
    fwd, back = fwd_ref[...], back_ref[...]
    total = groups * e_dev
    wide = count
    for i in range(0, count, wide):
        a = less_ref[:, (first + i) * orbitals : (first + i + wide) * orbitals]
        b = dot(fwd, gathered(great, i, wide))
        real = a[:freq] * b[:freq] + a[freq:] * b[freq:]
        imag = a[freq:] * b[:freq] - a[:freq] * b[freq:]
        pol = inverse(back, jnp.concatenate([real, imag], axis=0))
        for h in range(wide):
            scratch[pl.ds(i + h, total, stride=count), :] = pol[
                :, h * orbitals : (h + 1) * orbitals
            ]
    lags = e_dev // halves

    def part(d, h):
        start = (d * halves + h) * lags * count
        return scratch[start : start + lags * count, :].astype(BF16).reshape(lags, count, orbitals)

    for d in range(groups):
        outs[d][...] = part(d, 0)
        for h in range(1, halves):
            out = outs[h * groups + d]
            at = 0
            for ref in before[(h - 1) * groups + d :: (halves - 1) * groups]:
                out[:, at : at + ref.shape[1], :] = ref[...]
                at += ref.shape[1]
            out[:, at:, :] = part(d, h)


def sigma_kernel(groups, first, offsets, fwd_l_ref, back_ref, less_ref, *refs):
    halves = len(offsets)
    inter, outs = refs[: groups * halves], refs[groups * halves :]
    count, e_dev, orbitals = outs[0].shape
    freq = fwd_l_ref.shape[0] // 2
    fwd_l, back = fwd_l_ref[...], back_ref[...]
    inter = [
        inter[h * groups + d].at[offsets[h] : offsets[h] + count]
        for d in range(groups)
        for h in range(halves)
    ]
    wide = count
    for i in range(0, count, wide):
        a = less_ref[:, (first + i) * orbitals : (first + i + wide) * orbitals]
        b = dot(fwd_l, gathered(inter, i, wide))
        real = a[:freq] * b[:freq] - a[freq:] * b[freq:]
        imag = a[freq:] * b[:freq] + a[:freq] * b[freq:]
        sigma = inverse(back, jnp.concatenate([real, imag], axis=0)).astype(BF16)
        for h in range(wide):
            for d in range(groups):
                outs[d][i + h] = sigma[
                    d * e_dev : (d + 1) * e_dev, h * orbitals : (h + 1) * orbitals
                ]


def assemble_kernel(groups, *refs):
    out = refs[-1]
    ins = [part for d in range(groups) for part in refs[d:-1:groups]]
    at = 0
    for part in ins:
        out[:, at : at + part.shape[1], :] = part[...]
        at += part.shape[1]


def diagonal(a, b):
    zero = jnp.zeros_like(a)
    return jnp.concatenate(
        [jnp.concatenate([a, zero], axis=1), jnp.concatenate([zero, b], axis=1)], axis=0
    )


def setup_kernel(groups, count, me_ref, odd_ref, mask_ref, v_ref, *refs):
    sources, outs = refs[:count], refs[count : 2 * count]
    left, pair_right, far_right, scratch, sems = refs[2 * count :]
    me = me_ref[0]
    copies = [
        pltpu.make_async_copy(src.at[me], dst, sems.at[n])
        for n, (src, dst) in enumerate(zip(sources, outs))
    ]
    for copy in copies:
        copy.start()
    odd = odd_ref[0]
    scratch[0] = v_ref[1].astype(F32).T
    scratch[1] = v_ref[2 - 2 * odd].astype(F32).T
    scratch[2] = v_ref[2 * odd].astype(F32).T
    rows = scratch.shape[1] // groups

    def ordered(n):
        parts = [
            scratch[n, pl.ds(pl.multiple_of((me ^ d) * rows, rows), rows), :] for d in range(groups)
        ]
        return jnp.concatenate(parts, axis=0).T.astype(BF16)

    def masked(n, t):
        return (scratch[n] * mask_ref[t].astype(F32)).astype(BF16)

    left[...] = jnp.concatenate([ordered(0), ordered(1), ordered(2)], axis=1)
    pair_right[...] = diagonal(scratch[0].astype(BF16), masked(1, 1 - odd))
    far_right[...] = masked(2, odd)
    for copy in copies:
        copy.wait()


def screen_kernel(groups, me_ref, left, pair_right, far_right, own, near, far, *refs):
    outs, scratch = refs[:-1], refs[-1]
    lags, n, _ = far.shape
    rows = n // groups
    me = me_ref[0]
    both = jnp.concatenate([own[...].reshape(lags * n, n), near[...].reshape(lags * n, n)], axis=1)
    half = dot(both, pair_right[...]).astype(BF16)
    other = dot(far[...].reshape(lags * n, n), far_right[...]).astype(BF16)
    half = jnp.concatenate(
        [
            jnp.concatenate(
                [
                    half[k * n : k * n + n, :n],
                    half[k * n : k * n + n, n:],
                    other[k * n : k * n + n],
                ],
                axis=0,
            )
            for k in range(lags)
        ],
        axis=1,
    )
    terms = dot(left[...], half)
    for k in range(lags):
        scratch[pl.ds(k, n, stride=lags), :] = terms[:, k * n : k * n + n]
    first = 0
    for c in range(0, len(outs), groups):
        count = outs[c].shape[0]
        for d in range(groups):
            start = pl.multiple_of(((me ^ d) * rows + first) * lags, 8)
            part = scratch[pl.ds(start, count * lags), :]
            outs[c + d][...] = part.astype(BF16).reshape(count, lags, n)
        first += count


def final_kernel(groups, pieces, me_ref, *refs):
    ins, out = refs[: len(pieces)], refs[-len(pieces) - 2]
    scratch, sems = refs[-len(pieces) - 1 : -1], refs[-1]
    me = me_ref[0]
    copies = []
    for n, (d, first) in enumerate(pieces):
        count, e_dev, orbitals = ins[n].shape
        rows = orbitals // groups
        for i in range(count):
            scratch[n][pl.ds(i, e_dev, stride=count), :] = ins[n][i].astype(F32)
        start = pl.multiple_of((me ^ d) * rows + first, 8)
        copies.append(
            pltpu.make_async_copy(
                scratch[n].reshape(e_dev, count, orbitals),
                out.at[:, pl.ds(start, count), :],
                sems.at[n],
            )
        )
        copies[-1].start()
    for copy in copies:
        copy.wait()


def exchange(parts):
    groups = lax.axis_size("energy")
    moved = [parts[0]]
    for d in range(1, groups):
        moved.append(lax.ppermute(parts[d], "energy", [(i, i ^ d) for i in range(groups)]))
    return moved


def call(kernel, out_shape, specs, *args, scratch=(), **kwargs):
    return pl.pallas_call(
        kernel,
        out_shape=out_shape,
        in_specs=specs,
        scratch_shapes=list(scratch),
        compiler_params=params(),
        **kwargs,
    )(*args)


def shards(g_less, g_great, coupling, coupling_mask):
    e_dev, _, orbitals, _ = g_less.shape
    groups = lax.axis_size("energy")
    peers = lax.axis_size("block")
    rows = orbitals // groups
    total = e_dev * groups
    halves = 2 if e_dev % 32 == 0 else 1
    lags = e_dev // halves
    index = lax.axis_index("energy")
    me = index.astype(jnp.int32)[None]
    odd = (lax.axis_index("block") % 2).astype(jnp.int32)[None]
    smem = pl.BlockSpec(memory_space=pltpu.SMEM)
    hbm = pl.BlockSpec(memory_space=pltpu.HBM)

    def shape(*dims, dtype=BF16):
        return jax.ShapeDtypeStruct(dims, dtype)

    less = g_less.reshape(e_dev, orbitals, orbitals)
    great = g_great.reshape(e_dev, orbitals, orbitals)
    less, great = [pltpu.with_memory_space_constraint(x, pltpu.HBM) for x in (less, great)]

    parts = [shape(e_dev, rows, orbitals)] * groups
    less = call(
        functools.partial(slice_kernel, groups),
        parts,
        [smem, hbm],
        me,
        less,
        out_specs=[vmem()] * groups,
        scratch=[pltpu.SemaphoreType.DMA((groups,))],
    )
    less = exchange(less)
    stacks = [pltpu.with_memory_space_constraint(jnp.asarray(t), pltpu.HBM) for t in tables(groups, e_dev)]
    square = (orbitals, orbitals)
    fwd_e, fwd_l, back_l, back_e, left, pair_right, far_right = call(
        functools.partial(setup_kernel, groups, len(stacks)),
        [shape(*t.shape[1:]) for t in stacks]
        + [shape(orbitals, 3 * orbitals), shape(2 * orbitals, 2 * orbitals), shape(*square)],
        [smem, smem, smem, vmem()] + [hbm] * len(stacks),
        me,
        odd,
        coupling_mask[0],
        coupling[0],
        *stacks,
        out_specs=[vmem()] * (len(stacks) + 3),
        scratch=[pltpu.VMEM((3, *square), F32), pltpu.SemaphoreType.DMA((len(stacks),))],
    )
    counts = [rows // 2, rows // 2] if rows % 32 == 0 else [rows]
    parts = call(
        functools.partial(turn_kernel, groups, counts),
        [shape(count, e_dev, orbitals) for count in counts for _ in range(groups)],
        [smem, hbm],
        me,
        great,
        out_specs=[vmem()] * (groups * len(counts)),
        scratch=[
            pltpu.VMEM((e_dev, orbitals, orbitals), BF16),
            pltpu.VMEM((orbitals * e_dev, orbitals), F32),
            pltpu.SemaphoreType.DMA((8,)),
        ],
    )
    great = [exchange(parts[:groups])]
    rest = parts[groups:]
    less = call(
        spectrum_kernel,
        shape(fwd_e.shape[0], rows * orbitals, dtype=F32),
        [vmem()] * (1 + groups),
        fwd_e,
        *less,
        out_specs=vmem(),
        scratch=[pltpu.VMEM((total * rows, orbitals), F32)],
    )
    if len(counts) > 1:
        *rest, less = lax.optimization_barrier((*rest, less))
        great.append(exchange(rest))
    pol = [[] for _ in range(halves)]
    later = []
    for c, count in enumerate(counts):
        width = rows if c == len(counts) - 1 else count
        parts = call(
            functools.partial(pol_kernel, groups, halves, sum(counts[:c]), len(later)),
            [shape(lags, count, orbitals)] * groups
            + [shape(lags, width, orbitals)] * ((halves - 1) * groups),
            [vmem()] * (3 + groups + len(later)),
            fwd_e,
            back_l,
            less,
            *great[c],
            *later,
            out_specs=[vmem()] * (halves * groups),
            scratch=[pltpu.VMEM((total * count, orbitals), F32)],
        )
        pol[0].append(exchange(parts[:groups]))
        later += parts[groups:]
    for h in range(1, halves):
        last = len(later) - (halves - h) * groups
        pol[h].append(exchange(later[last : last + groups]))

    near_pairs = [(b, b ^ 1) for b in range(peers) if b ^ 1 < peers]
    far_pairs = [(b, ((b + 1) ^ 1) - 1) for b in range(1, peers) if ((b + 1) ^ 1) - 1 < peers]
    inter = []
    for h in range(halves):
        parts = [part for chunk in pol[h] for part in chunk]
        own = call(
            functools.partial(assemble_kernel, groups),
            shape(lags, orbitals, orbitals),
            [vmem()] * len(parts),
            *parts,
            out_specs=vmem(),
        )
        far = lax.ppermute(own, "block", far_pairs)
        near = lax.ppermute(own, "block", near_pairs)
        parts = call(
            functools.partial(screen_kernel, groups),
            [shape(rows, lags, orbitals)] * groups,
            [smem] + [vmem()] * 6,
            me,
            left,
            pair_right,
            far_right,
            own,
            near,
            far,
            out_specs=[vmem()] * groups,
            scratch=[pltpu.VMEM((orbitals * lags, orbitals), F32)],
        )
        inter.append(exchange(parts))

    counts = [3 * rows // 4, rows // 4] if rows % 32 == 0 else [rows]
    sigma = []
    for c, count in enumerate(counts):
        first = sum(counts[:c])
        parts = call(
            functools.partial(sigma_kernel, groups, first, [first] * halves),
            [shape(count, e_dev, orbitals)] * groups,
            [vmem()] * (3 + groups * halves),
            fwd_l,
            back_e,
            less,
            *[part for half in inter for part in half],
            out_specs=[vmem()] * groups,
        )
        sigma.append((first, count, exchange(parts)))
    pieces = [[(d, first, part) for d, part in enumerate(parts)] for first, _, parts in sigma]
    if len(pieces) > 1:
        pieces[-2].append(pieces[-1].pop(0))
    out = []
    for group in pieces:
        out = [
            call(
                functools.partial(final_kernel, groups, [(d, first) for d, first, _ in group]),
                shape(e_dev, orbitals, orbitals, dtype=F32),
                [smem] + [vmem()] * len(group) + [hbm] * len(out),
                me,
                *[part for _, _, part in group],
                *out,
                out_specs=hbm,
                scratch=[
                    pltpu.VMEM((e_dev * part.shape[0], orbitals), F32) for _, _, part in group
                ]
                + [pltpu.SemaphoreType.DMA((len(group),))],
                input_output_aliases={1 + len(group): 0} if out else {},
            )
        ]
    return out[0].reshape(e_dev, 1, orbitals, orbitals)


def solution(mesh):
    return jax.shard_map(
        shards,
        mesh=mesh,
        in_specs=(
            P("energy", "block", None, None),
            P("energy", "block", None, None),
            P("block", None, None, None),
            P("block", None),
        ),
        out_specs=P("energy", "block", None, None),
        check_vma=False,
    )
```
